256 devices in a mesh: tile: 32 (over x, y, core), lev: 8 (over z).
Axes of the slice: x: 4, y: 4, z: 8, core: 2. Of those that a mesh axis runs over, the one named last changes fastest.
Arguments:
- field: float32 [32, 40, 256, 256], P('tile', 'lev'), may hold values from -6 to 6
- kappa_x: float32 [32, 256, 256], P('tile'), may hold values from 0.04 to 0.12
- kappa_y: float32 [32, 256, 256], P('tile'), may hold values from 0.04 to 0.12
- sea_mask: int32 [32, 256, 256], P('tile'), may hold values 0 or 1
- tile_links: int32 [32, 4], P('tile'), may hold values from -1 to 127, as said below
- vertical: bfloat16 [40, 40], replicated, may hold values from -1 to 1
Outputs:
- correlated: float32 [32, 40, 256, 256], P('tile', 'lev')
The draws below stay inside these ranges and needn't reach their ends.
Inputs may be any that keep to these rules, and one draw needn't show every extreme that they name: `tile_links`: tile n lies in column n of a single row of G = 32 columns that wraps east-west. West and east links go to the same row of the previous and next column (to its east and west face), no tile has a south link, and the north link of every tile is always present and goes to the top-row tile of column (G - c) % G, to its north face. A link of tile n to tile m is present exactly when the matching link of m to n is.
All inputs are finite; a program needn't handle non-finite values. No bound on the sum of `sea_mask` on one device may be relied on, other than what follows from the above.
Results may differ from the reference program's by a relative error of at most 0.0029.
Values may be sent and summed in bfloat16 or wider, within the bound.
No kernel may reach another device: no remote copies, remote signals or barrier semaphores. Data moves between devices by JAX's collectives and lax.ppermute only.
A program may use at most 128 MiB of HBM per device.

```python
import jax
import jax.numpy as jnp
from jax import lax

TS = 256
TPD = 1
STEPS = 10
TILES = 32
NLEV = 40


def draw_tile_links(key, part):
    key = jax.random.fold_in(key, 7)
    grid_columns = TILES // TPD
    east_open = jax.random.randint(jax.random.fold_in(key, 1), (grid_columns, TPD), 0, 20) >= 3
    north_open = jax.random.randint(jax.random.fold_in(key, 2), (grid_columns, TPD), 0, 20) >= 3
    tile_ids = jnp.arange(TILES, dtype=jnp.int32)
    column = tile_ids // TPD
    tile_row = tile_ids % TPD
    west_column = (column - 1) % grid_columns
    east_column = (column + 1) % grid_columns
    mirror = (grid_columns - column) % grid_columns
    west_link = jnp.where(east_open[west_column, tile_row], 4 * (west_column * TPD + tile_row) + 1, -1)
    east_link = jnp.where(east_open[column, tile_row], 4 * (east_column * TPD + tile_row), -1)
    below = jnp.maximum(tile_row - 1, 0)
    south_link = jnp.where((tile_row > 0) & north_open[column, below], 4 * (tile_ids - 1) + 3, -1)
    top_row = tile_row == TPD - 1
    inner_north = jnp.where(north_open[column, tile_row], 4 * (tile_ids + 1) + 2, -1)
    fold_north = 4 * (mirror * TPD + tile_row) + 3
    north_link = jnp.where(top_row, fold_north, inner_north)
    return jnp.stack([west_link, east_link, south_link, north_link], axis=1).astype(jnp.int32)


def with_ends(values, rng, least, top_value):
    extent = values.shape
    spot = [jax.random.randint(jax.random.fold_in(rng, axis), (), 0, extent[axis]) for axis in range(len(extent))]
    values = values.at[tuple(spot)].set(least)
    longest = extent.index(max(extent))
    spot[longest] = (spot[longest] + 1) % extent[longest]
    return values.at[tuple(spot)].set(top_value)


def shard_levels(own_key, extent, cuts, low, high):
    loudness = 1.0
    for dim, blocks in cuts:
        heights = jax.random.uniform(jax.random.fold_in(jax.random.fold_in(own_key, 6), dim), (blocks,), jnp.float32, low / len(cuts), high / len(cuts))
        loudness = loudness * jnp.repeat(jnp.exp(heights), extent[dim] // blocks).reshape((-1,) + (1,) * (len(extent) - 1 - dim))
    return loudness


def bell_draw(key, extent, spread, reach, cuts=(), kind=jnp.bfloat16):
    gain = shard_levels(key, extent, cuts, -0.22, 0.18) if cuts else 1.0
    entries = jax.random.normal(key, extent, jnp.float32) * spread * gain
    return jnp.minimum(jnp.maximum(entries, -reach), reach).astype(kind)


def setup_inputs(seed: int = 0) -> dict:
    streams_of = jax.random.split(jax.random.key(seed), 7)
    return {
        "field": bell_draw(streams_of[0], (TILES, NLEV, TS, TS), 1.0, 6.0, ((0, 32), (1, 8)), jnp.float32),
        "kappa_x": jnp.clip(0.04 + 0.08 * jax.random.uniform(streams_of[1], (TILES, TS, TS), jnp.float32) ** shard_levels(streams_of[1], (TILES, TS, TS), ((0, 32),), -0.2, 0.2), 0.04, 0.12),
        "kappa_y": jnp.clip(0.04 + 0.08 * jax.random.uniform(streams_of[2], (TILES, TS, TS), jnp.float32) ** shard_levels(streams_of[2], (TILES, TS, TS), ((0, 32),), -0.2, 0.2), 0.04, 0.12),
        "sea_mask": with_ends((jax.random.randint(streams_of[3], (TILES, TS, TS), 0, 20) < 17).astype(jnp.int32), jax.random.fold_in(streams_of[3], 1), 0, 1),
        "tile_links": draw_tile_links(jax.random.fold_in(streams_of[6], 71), 0),
        "vertical": bell_draw(streams_of[5], (NLEV, NLEV), NLEV ** -0.5, 1.0),
    }


def faces_of(values):
    return jnp.stack([values[..., :, 0], values[..., :, -1], values[..., 0, :], values[..., -1, :]], axis=1)


def place(fetched, linked, reverse):
    trailing = (1,) * (fetched.ndim - 2)
    fetched = jnp.where(reverse.reshape(reverse.shape + trailing), jnp.flip(fetched, -1), fetched)
    return jnp.where(linked.reshape(linked.shape + trailing), fetched, jnp.zeros_like(fetched))


def neighbours(values, rim_cells):
    west_cells = jnp.concatenate([rim_cells[:, 0, ..., None], values[..., :, :-1]], axis=-1)
    east_cells = jnp.concatenate([values[..., :, 1:], rim_cells[:, 1, ..., None]], axis=-1)
    south_cells = jnp.concatenate([rim_cells[:, 2, ..., None, :], values[..., :-1, :]], axis=-2)
    north_cells = jnp.concatenate([values[..., 1:, :], rim_cells[:, 3, ..., None, :]], axis=-2)
    return west_cells, east_cells, south_cells, north_cells


def pair_weights(statics, rim_cells):
    west_cells, east_cells, south_cells, north_cells = neighbours(statics, rim_cells)
    sea_cells = statics[:, 0]
    to_west = 0.5 * (statics[:, 1] + west_cells[:, 1]) * sea_cells * west_cells[:, 0]
    to_east = 0.5 * (statics[:, 1] + east_cells[:, 1]) * sea_cells * east_cells[:, 0]
    to_south = 0.5 * (statics[:, 2] + south_cells[:, 2]) * sea_cells * south_cells[:, 0]
    to_north = 0.5 * (statics[:, 2] + north_cells[:, 2]) * sea_cells * north_cells[:, 0]
    return to_west, to_east, to_south, to_north


def diffuse(current, rim_cells, weights):
    west_cells, east_cells, south_cells, north_cells = neighbours(current, rim_cells)
    to_west, to_east, to_south, to_north = weights
    return current + (to_west * (west_cells - current) + to_east * (east_cells - current)
                      + to_south * (south_cells - current) + to_north * (north_cells - current))


def reference(field, kappa_x, kappa_y, sea_mask, tile_links, vertical):
    sea_cells = sea_mask.astype(jnp.float32)
    side_ids = jnp.arange(4, dtype=jnp.int32)[None, :]
    linked = tile_links >= 0
    reverse = linked & (tile_links % 4 == side_ids)
    position = jnp.where(linked, tile_links, 0).astype(jnp.int32)

    def rims_of(values):
        tile_faces = faces_of(values)
        face_pool = tile_faces.reshape((-1,) + tile_faces.shape[2:])
        return place(jnp.take(face_pool, position, axis=0), linked, reverse)

    statics = jnp.stack([sea_cells, kappa_x, kappa_y], axis=1)
    weights = pair_weights(statics, rims_of(statics))

    def one_level(level_field):
        current = level_field * sea_cells
        for _ in range(STEPS):
            current = diffuse(current, rims_of(current), weights)
        return current.astype(jnp.bfloat16)

    smooth = jnp.moveaxis(lax.map(one_level, jnp.moveaxis(field, 1, 0)), 0, 1)

    def one_tile(levels):
        flat_cells = levels.reshape(levels.shape[0], -1)
        return jnp.dot(vertical, flat_cells, preferred_element_type=jnp.float32).reshape(levels.shape)

    return lax.map(one_tile, smooth)
```

```python
import jax
import jax.numpy as jnp
from jax import lax
from jax.experimental import pallas as pl
from jax.experimental.pallas import tpu as pltpu
from jax.sharding import PartitionSpec as P

STEPS = 10
LEV = 5
PLANES = LEV + 3
SIDE = 256
ROWS = 32
HALO = 12
DEPTH = 10
STRIP = ROWS + DEPTH
TOP = 24
NORTH = 5
CHUNKS = 8

VMEM = pl.BlockSpec(memory_space=pltpu.VMEM)
SMEM = pl.BlockSpec(memory_space=pltpu.SMEM)


def lanes():
    return lax.broadcasted_iota(jnp.int32, (8, 128), 1)


def sublanes():
    return lax.broadcasted_iota(jnp.int32, (8, 128), 0)


def roll(x, shift):
    shift = shift % 128
    return x if shift == 0 else pltpu.roll(x, shift, 1)


def up(x):
    return pltpu.roll(x, 7, 0)


def down(x):
    return pltpu.roll(x, 1, 0)


def strided(halves, lead, t, half, stride):
    return halves[half][(*lead, pl.ds(t, 8, stride=stride), slice(None))]


def half_specs(*leads):
    return [
        pl.BlockSpec((*lead, SIDE, 128), lambda i, n=len(lead), h=h: (0,) * (n + 1) + (h,))
        for lead in leads
        for h in range(2)
    ]


def doubled(*arrays):
    return [a for a in arrays for _ in range(2)]


def paired(refs):
    return [refs[i : i + 2] for i in range(0, len(refs), 2)]


def planes_at(field, kx, ky, sea, t, half):
    land = strided(sea, (), t, half, ROWS).astype(jnp.float32)
    out = [strided(field, (l,), t, half, ROWS) * land for l in range(LEV)]
    return out + [land, strided(kx, (), t, half, ROWS), strided(ky, (), t, half, ROWS)]


def pack_kernel(links, *refs):
    field, kx, ky, sea = paired(refs[:8])
    west, east, north, nw, ne, rows = refs[8:]
    lane = lanes()
    group = lane // 16
    for t in range(ROWS):
        low = planes_at(field, kx, ky, sea, t, 0)
        high = planes_at(field, kx, ky, sea, t, 1)
        w, e = low[0], roll(high[0], 16)
        for p in range(1, PLANES):
            w = jnp.where(group == p, roll(low[p], 16 * p), w)
            e = jnp.where(group == p, roll(high[p], 16 * p + 16), e)
        west[8 * t : 8 * t + 8, :] = w
        east[8 * t : 8 * t + 8, :] = e
    flip = 127 - lane
    for p in range(PLANES):
        for o in range(2):
            for half in range(2):
                at = pl.ds(SIDE - 16 + 8 * o, 8)
                if p <= LEV:
                    x = sea[half][at, :].astype(jnp.float32)
                    x = field[half][p, at, :] * x if p < LEV else x
                else:
                    x = (kx, ky)[p - LEV - 1][half][at, :]
                x = jnp.take_along_axis(x, flip, axis=1)
                rows[p, 8 * o : 8 * o + 8, 128 * (1 - half) : 128 * (1 - half) + 128] = x
    for k in range(16):
        north[:, k, :] = rows[:, 15 - k, :]
    west_open = jnp.where(links[0, 0] >= 0, 1.0, 0.0).astype(jnp.float32)
    east_open = jnp.where(links[0, 1] >= 0, 1.0, 0.0).astype(jnp.float32)
    north[LEV, 14, :] = jnp.full((SIDE,), 1.0, jnp.float32) * west_open
    north[LEV, 15, :] = jnp.full((SIDE,), 1.0, jnp.float32) * east_open
    swap = jnp.bitwise_xor(lane, 15)
    for k in range(16):
        r = 8 * (ROWS - 1 - k) + 7
        nw[k : k + 1, :] = west[r : r + 1, :]
        ne[k : k + 1, :] = east[r : r + 1, :]
    for o in range(2):
        nw[8 * o : 8 * o + 8, :] = jnp.take_along_axis(nw[8 * o : 8 * o + 8, :], swap, axis=1)
        ne[8 * o : 8 * o + 8, :] = jnp.take_along_axis(ne[8 * o : 8 * o + 8, :], swap, axis=1)


def pack(links, field, kx, ky, sea):
    f32 = jnp.float32
    shapes = [(SIDE, 128), (SIDE, 128), (PLANES, 16, SIDE), (16, 128), (16, 128)]
    return pl.pallas_call(
        pack_kernel,
        out_shape=[jax.ShapeDtypeStruct(s, f32) for s in shapes],
        grid=(1,),
        in_specs=[SMEM] + half_specs((LEV,), (), (), ()),
        out_specs=[VMEM] * 5,
        scratch_shapes=[pltpu.VMEM((PLANES, 16, SIDE), f32)],
        compiler_params=pltpu.CompilerParams(vmem_limit_bytes=60 << 20),
        name="pack",
    )(links, *doubled(field, kx, ky, sea))


def wide_weights(sea, kx, ky, rows, we, ww, wn):
    lane, sub = lanes(), sublanes()
    for t in range(rows):
        s = [sea(t, h) for h in range(2)]
        x = [kx(t, h) for h in range(2)]
        se = [jnp.where(lane == 127, roll(s[1], -1), roll(s[0], -1)), roll(s[1], -1)]
        xe = [jnp.where(lane == 127, roll(x[1], -1), roll(x[0], -1)), roll(x[1], -1)]
        shifted = []
        for h in range(2):
            w = 0.5 * (x[h] + xe[h]) * s[h] * se[h]
            if h == 1:
                w = jnp.where(lane == 127, 0.0, w)
            we[t, :, 128 * h : 128 * h + 128] = w
            shifted.append(roll(w, 1))
            if t < rows - 1:
                sn, yn = sea(t + 1, h), ky(t + 1, h)
            else:
                sn, yn = up(sea(0, h)), up(ky(0, h))
            w = 0.5 * (ky(t, h) + yn) * s[h] * sn
            if t == rows - 1:
                w = jnp.where(sub == 7, 0.0, w)
            wn[t, :, 128 * h : 128 * h + 128] = w
        ww[t, :, 0:128] = jnp.where(lane == 0, 0.0, shifted[0])
        ww[t, :, 128:256] = jnp.where(lane == 0, shifted[0], shifted[1])


HALVES = (slice(0, 128), slice(128, 256))


def wide_step(src, dst, we, ww, wn, rows, levels, block):
    lane = lanes()
    first, last = lane == 0, lane == 127
    below = []
    for l in levels:
        for h in HALVES:
            over = up(src[l, 0, :, h])
            src[l, rows, :, h] = over
            below.append(down(wn[rows - 1, :, h] * (over - src[l, rows - 1, :, h])))

    def body(b, below):
        here = [src[l, b * block, :, h] for l in levels for h in HALVES]
        for j in range(block):
            t = b * block + j
            e = [we[t, :, h] for h in HALVES]
            w = [ww[t, :, h] for h in HALVES]
            n = [wn[t, :, h] for h in HALVES]
            nxt = [src[l, t + 1, :, h] for l in levels for h in HALVES]
            flux = [n[i % 2] * (nxt[i] - here[i]) for i in range(len(here))]
            for i, l in zip(range(0, len(here), 2), levels):
                lo, hi = here[i : i + 2]
                e_lo, e_hi = roll(lo, -1), roll(hi, -1)
                w_lo, w_hi = roll(lo, 1), roll(hi, 1)
                x_lo = e[0] * (jnp.where(last, e_hi, e_lo) - lo) + w[0] * (w_lo - lo)
                x_hi = e[1] * (e_hi - hi) + w[1] * (jnp.where(first, w_lo, w_hi) - hi)
                dst[l, t, :, HALVES[0]] = lo + x_lo + (flux[i] - below[i])
                dst[l, t, :, HALVES[1]] = hi + x_hi + (flux[i + 1] - below[i + 1])
            here, below = nxt, flux
        return tuple(below)

    if rows == block:
        body(0, below)
    else:
        lax.fori_loop(0, rows // block, body, tuple(below))


def mixing(vertical):
    levels = vertical.shape[0]
    size = 16 * levels

    def at(shape, axis):
        return lax.broadcasted_iota(jnp.int32, shape, axis)

    left = (at((size, levels), 0) // 16 == at((size, levels), 1)).astype(jnp.float32).astype(jnp.bfloat16)
    right = (at((levels, size), 1) // 16 == at((levels, size), 0)).astype(jnp.float32).astype(jnp.bfloat16)
    tall = jnp.dot(left, vertical, preferred_element_type=jnp.float32).astype(jnp.bfloat16)
    full = jnp.dot(tall, right, preferred_element_type=jnp.float32)
    same = at((size, size), 0) % 16 == at((size, size), 1) % 16
    return jnp.where(same, full, 0.0).astype(jnp.bfloat16)


def inner_kernel(*refs):
    field, kx, ky, sea = paired(refs[:8])
    vertical, cur, own, statics, top, mixer, other, we, ww, wn = refs[8:]
    lane = lanes()
    group = lane // 32

    def plane(ref):
        return lambda t, h: strided(ref, (), t, h, ROWS).astype(jnp.float32)

    wide_weights(plane(sea), plane(kx), plane(ky), ROWS, we, ww, wn)
    for t in range(ROWS):
        low = planes_at(field, kx, ky, sea, t, 0)
        high = planes_at(field, kx, ky, sea, t, 1)
        for l in range(LEV):
            cur[l, t, :, 0:128] = low[l]
            cur[l, t, :, 128:256] = high[l]
        a, b = roll(low[0], HALO), roll(high[0], -108)
        for l in range(1, 4):
            a = jnp.where(group == l, roll(low[l], HALO + 32 * l), a)
            b = jnp.where(group == l, roll(high[l], 32 * l - 108), b)
        own[0, t] = a
        own[1, t] = b
        own[2, t] = jnp.where(group == 0, roll(low[4], HALO), roll(high[4], 32 - 108))
        for p in range(3):
            statics[p, t] = jnp.where(group == 0, roll(low[LEV + p], HALO), roll(high[LEV + p], 32 - 108))
    for h in range(2):
        land = sea[h][SIDE - TOP :, :].astype(jnp.float32)
        for l in range(LEV):
            top[h, l] = field[h][l, SIDE - TOP :, :] * land
        top[h, LEV] = land
        top[h, LEV + 1] = kx[h][SIDE - TOP :, :]
        top[h, LEV + 2] = ky[h][SIDE - TOP :, :]

    mixer[...] = mixing(vertical[...])

    def two_steps(_, none):
        wide_step(cur, other, we, ww, wn, ROWS, range(LEV), 8)
        wide_step(other, cur, we, ww, wn, ROWS, range(LEV), 8)
        return none

    lax.fori_loop(0, STEPS // 2, two_steps, 0)


def inner(field, kx, ky, sea, vertical):
    f32 = jnp.float32
    shapes = [(LEV, ROWS + 1, 8, SIDE), (3, ROWS, 8, 128), (3, ROWS, 8, 128), (2, PLANES, TOP, 128)]
    return pl.pallas_call(
        inner_kernel,
        out_shape=[jax.ShapeDtypeStruct(s, f32) for s in shapes] + [jax.ShapeDtypeStruct((640, 640), jnp.bfloat16)],
        grid=(1,),
        in_specs=half_specs((LEV,), (), (), ()) + [VMEM],
        out_specs=[VMEM] * 5,
        scratch_shapes=[pltpu.VMEM((LEV, ROWS + 1, 8, SIDE), f32)] + [pltpu.VMEM((ROWS, 8, SIDE), f32)] * 3,
        compiler_params=pltpu.CompilerParams(vmem_limit_bytes=24 << 20),
        cost_estimate=pl.CostEstimate(flops=40_000_000, bytes_accessed=40_000_000, transcendentals=0),
        name="inner",
    )(*doubled(field, kx, ky, sea), vertical)


def strip_step(src, dst, we, ww, wn, tiles, block):
    sub = sublanes()
    below = []
    for k in tiles:
        over = jnp.where(sub == 7, src[k, ROWS], up(src[k, 0]))
        src[k, ROWS] = over
        below.append(jnp.where(sub == 0, 0.0, down(wn[k, ROWS - 1] * (over - src[k, ROWS - 1]))))

    def body(b, below):
        here = [src[k, b * block] for k in tiles]
        for j in range(block):
            t = b * block + j
            nxt = [src[k, t + 1] for k in tiles]
            flux = [wn[k, t] * (n - c) for k, n, c in zip(tiles, nxt, here)]
            for k, c, f, g in zip(tiles, here, flux, below):
                x = we[k, t] * (roll(c, -1) - c) + ww[k, t] * (roll(c, 1) - c)
                dst[k, t] = c + x + (f - g)
            here, below = nxt, flux
        return tuple(below)

    lax.fori_loop(0, STRIP // block, body, tuple(below))


def rim_kernel(links, inside, own, statics, top, west, east, north, nw, ne, out, cur, other, we, ww, wn, nb_west, nb_east, nc, n_other, nwe, nww, nwn, st):
    lane, sub = lanes(), sublanes()
    group, part = lane // 32, lane % 32
    w_halo, e_halo = part < HALO, part >= 20
    ones = jnp.ones((8, 128), jnp.float32)

    for t in range(STRIP):
        if t < ROWS:
            w, e = west[8 * t : 8 * t + 8, :], east[8 * t : 8 * t + 8, :]
            a, b, c = own[0, t], own[1, t], own[2, t]
            s = [statics[p, t] for p in range(3)]
        else:
            k = t - ROWS
            w = jnp.broadcast_to(nw[k : k + 1, :], (8, 128))
            e = jnp.broadcast_to(ne[k : k + 1, :], (8, 128))
            low = [jnp.broadcast_to(north[p, k : k + 1, 0:128], (8, 128)) for p in range(PLANES)]
            high = [jnp.broadcast_to(north[p, k : k + 1, 128:256], (8, 128)) for p in range(PLANES)]
            a, b = roll(low[0], HALO), roll(high[0], -108)
            for l in range(1, 4):
                a = jnp.where(group == l, roll(low[l], HALO + 32 * l), a)
                b = jnp.where(group == l, roll(high[l], 32 * l - 108), b)
            c = jnp.where(group == 0, roll(low[4], HALO), roll(high[4], 32 - 108))
            s = [jnp.where(group == 0, roll(low[LEV + p], HALO), roll(high[LEV + p], 32 - 108)) for p in range(3)]
        for l in range(4):
            a = jnp.where(w_halo & (group == l), roll(w, 16 * l - 4), a)
            b = jnp.where(e_halo & (group == l), roll(e, 16 * l + 20), b)
        c = jnp.where(w_halo & (group == 0), roll(w, -68), c)
        c = jnp.where(e_halo & (group == 1), roll(e, 52 - 64), c)
        cur[0, t] = a
        cur[1, t] = b
        cur[2, t] = c
        for p in range(3):
            q = LEV + p
            x = jnp.where(w_halo & (group == 0), roll(w, -(16 * q + 4)), s[p])
            st[p, t] = jnp.where(e_halo & (group == 1), roll(e, 52 - 16 * q), x)

    def flag(x):
        return jnp.where(x >= 0, 1.0, 0.0).astype(jnp.float32)

    w_open = ones * flag(links[0, 0])
    e_open = ones * flag(links[0, 1])
    w_over = jnp.broadcast_to(north[LEV, 15:16, 0:128], (8, 128))
    e_over = jnp.broadcast_to(north[LEV, 14:15, 0:128], (8, 128))
    shut = part == 31
    w_seam, e_seam = lane == HALO - 1, lane == 32 + 19
    seams = []
    for a, b in ((w_open, e_open), (w_over, e_over)):
        m = jnp.where(w_seam, a, jnp.where(e_seam, b, 1.0))
        seams.append(0.5 * jnp.where(shut, 0.0, m))

    def spread(x):
        lo = jnp.where(group == 0, x, 0.0)
        hi = jnp.where(group == 1, x, 0.0)
        lo = lo + roll(lo, 32)
        hi = hi + roll(hi, 32)
        return lo + roll(lo, 64), hi + roll(hi, 64)

    for t in range(STRIP):
        s, x, y = st[0, t], st[1, t], st[2, t]
        w = seams[t >= ROWS] * (x + roll(x, -1)) * s * roll(s, -1)
        we[0, t], we[1, t] = spread(w)
        we[2, t] = w
        for i in range(3):
            ww[i, t] = roll(we[i, t], 1)
        if t < STRIP - 1:
            sn, yn = st[0, t + 1], st[2, t + 1]
            if t == ROWS - 1:
                sn = jnp.where(sub == 7, sn, up(st[0, 0]))
                yn = jnp.where(sub == 7, yn, up(st[2, 0]))
            w = 0.5 * (y + yn) * s * sn
            wn[0, t], wn[1, t] = spread(w)
            wn[2, t] = w

    zeros = jnp.zeros((8, 128), jnp.float32)
    for i in range(3):
        wn[i, STRIP - 1] = zeros
        cur[i, STRIP] = zeros
        other[i, STRIP] = zeros

    nb = (nb_west, nb_east)
    for h in range(2):
        nb[h][:, 0:TOP, :] = top[h]
        nb[h][:, TOP : TOP + 16, :] = north[:, :, 128 * h : 128 * h + 128]
    for l in range(LEV):
        for t in range(NORTH):
            for h in range(2):
                nc[l, t, :, 128 * h : 128 * h + 128] = strided(nb, (l,), t, h, NORTH)

    def plane(p):
        return lambda t, h: strided(nb, (p,), t, h, NORTH)

    wide_weights(plane(LEV), plane(LEV + 1), plane(LEV + 2), NORTH, nwe, nww, nwn)

    def two_steps(_, none):
        strip_step(cur, other, we, ww, wn, range(3), 14)
        wide_step(nc, n_other, nwe, nww, nwn, NORTH, range(LEV), NORTH)
        strip_step(other, cur, we, ww, wn, range(3), 14)
        wide_step(n_other, nc, nwe, nww, nwn, NORTH, range(LEV), NORTH)
        return none

    lax.fori_loop(0, STEPS // 2, two_steps, 0)

    for l in range(LEV):
        for t in range(NORTH):
            for h in range(2):
                nb[h][l, pl.ds(t, 8, stride=NORTH), :] = nc[l, t, :, 128 * h : 128 * h + 128]

    w_rim, e_rim = lane < 10, lane >= 118
    top_row = sub == 7
    for l in range(LEV):
        for t in range(0, ROWS, 2):
            pair = []
            for u in (t, t + 1):
                lo, hi = inside[l, u, :, 0:128], inside[l, u, :, 128:256]
                if u >= ROWS - DEPTH:
                    r = TOP - ROWS + u
                    lo = jnp.where(top_row, jnp.broadcast_to(nb[0][l, r : r + 1, :], (8, 128)), lo)
                    hi = jnp.where(top_row, jnp.broadcast_to(nb[1][l, r : r + 1, :], (8, 128)), hi)
                if l < 4:
                    w, e = roll(cur[0, u], -(32 * l + HALO)), roll(cur[1, u], 108 - 32 * l)
                else:
                    w, e = roll(cur[2, u], -HALO), roll(cur[2, u], 108 - 32)
                pair.append((jnp.where(w_rim, w, lo), jnp.where(e_rim, e, hi)))
            q, r = t // 4, 8 * (t % 4)
            for h in range(2):
                x = jnp.concatenate([pair[0][h], pair[1][h]], axis=0)
                out[q, l, r : r + 16, 128 * h : 128 * h + 128] = x.astype(jnp.bfloat16)


def rim(links, inside, own, statics, top, west, east, north, nw, ne):
    f32 = jnp.float32
    scratch = [
        (3, STRIP + 1, 8, 128),
        (3, STRIP + 1, 8, 128),
        (3, STRIP, 8, 128),
        (3, STRIP, 8, 128),
        (3, STRIP, 8, 128),
        (PLANES, TOP + 16, 128),
        (PLANES, TOP + 16, 128),
        (LEV, NORTH + 1, 8, SIDE),
        (LEV, NORTH + 1, 8, SIDE),
        (NORTH, 8, SIDE),
        (NORTH, 8, SIDE),
        (NORTH, 8, SIDE),
        (3, STRIP, 8, 128),
    ]
    return pl.pallas_call(
        rim_kernel,
        out_shape=jax.ShapeDtypeStruct((CHUNKS, LEV, SIDE // CHUNKS, SIDE), jnp.bfloat16),
        in_specs=[SMEM] + [VMEM] * 9,
        out_specs=VMEM,
        scratch_shapes=[pltpu.VMEM(s, f32) for s in scratch],
        compiler_params=pltpu.CompilerParams(vmem_limit_bytes=24 << 20),
        name="rim",
    )(links, inside, own, statics, top, west, east, north, nw, ne)


def mix_kernel(x, k, y):
    for h in range(2):
        rows = x[:, :, 16 * h : 16 * h + 16, :].reshape(CHUNKS * LEV * 16, SIDE)
        mixed = jnp.dot(k[...], rows, preferred_element_type=jnp.float32).astype(jnp.bfloat16)
        y[:, :, 16 * h : 16 * h + 16, :] = mixed.reshape(CHUNKS, LEV, 16, SIDE)


def mix(x, k):
    return pl.pallas_call(
        mix_kernel,
        out_shape=jax.ShapeDtypeStruct(x.shape, jnp.bfloat16),
        in_specs=[VMEM] * 2,
        out_specs=VMEM,
        compiler_params=pltpu.CompilerParams(vmem_limit_bytes=24 << 20),
        name="mix",
    )(x, k)


def unpack_kernel(z, out):
    for q in range(CHUNKS):
        for l in range(LEV):
            for r in range(0, 32, 16):
                x = z[q, l, r : r + 16, :].astype(jnp.float32)
                for u in range(2):
                    t = 4 * q + r // 8 + u
                    out[l, pl.ds(t, 8, stride=ROWS), :] = x[8 * u : 8 * u + 8]


def unpack(z):
    return pl.pallas_call(
        unpack_kernel,
        out_shape=jax.ShapeDtypeStruct((LEV, SIDE, SIDE), jnp.float32),
        grid=(2,),
        in_specs=[pl.BlockSpec((CHUNKS, LEV, SIDE // CHUNKS, 128), lambda h: (0, 0, 0, h))],
        out_specs=pl.BlockSpec((LEV, SIDE, 128), lambda h: (0, 0, h)),
        compiler_params=pltpu.CompilerParams(vmem_limit_bytes=24 << 20),
        name="unpack",
    )(z)


def shards(field, kappa_x, kappa_y, sea_mask, tile_links, vertical):
    tiles = lax.axis_size("tile")

    def send(x, target):
        return lax.ppermute(x, "tile", [(i, target(i) % tiles) for i in range(tiles)])

    cells, kx, ky, sea = field[0], kappa_x[0], kappa_y[0], sea_mask[0]
    west, east, north, nw, ne = pack(tile_links, cells, kx, ky, sea)
    from_east = send(west, lambda i: i - 1)
    from_west = send(east, lambda i: i + 1)
    from_north = send(north, lambda i: -i)
    from_nw = send(nw, lambda i: 1 - i)
    from_ne = send(ne, lambda i: -1 - i)
    inside, own, statics, top, mixer = inner(cells, kx, ky, sea, vertical)
    smooth = rim(tile_links, inside, own, statics, top, from_west, from_east, from_north, from_nw, from_ne)
    gathered = lax.all_to_all(smooth, "lev", 0, 0, tiled=True)
    back = lax.all_to_all(mix(gathered, mixer), "lev", 0, 0, tiled=True)
    return unpack(back)[None]


def solution(mesh):
    placed = (
        P("tile", "lev", None, None),
        P("tile", None, None),
        P("tile", None, None),
        P("tile", None, None),
        P("tile", None),
        P(),
    )
    return jax.shard_map(
        shards, mesh=mesh, in_specs=placed, out_specs=P("tile", "lev", None, None), check_vma=False
    )
```

```python
import jax
import jax.numpy as jnp
from jax import lax
from jax.experimental import pallas as pl
from jax.experimental.pallas import tpu as pltpu
from jax.sharding import PartitionSpec as P

STEPS = 10
LEV = 5
PLANES = LEV + 3
SIDE = 256
ROWS = 32
HALO = 12
DEPTH = 10
STRIP = ROWS + DEPTH
TOP = 24
NORTH = 5
CHUNKS = 8
SLOT = (0, 4, 2, 6, 1, 5, 3, 7)
TILES = ((0, 1), (2, 3), (4, 5), (6, 7))
W_SHIFT = (-4, -36, -20, -52)
E_SHIFT = (52, 20, 36, 4)

VMEM = pl.BlockSpec(memory_space=pltpu.VMEM)
SMEM = pl.BlockSpec(memory_space=pltpu.SMEM)


def lanes():
    return lax.broadcasted_iota(jnp.int32, (8, 128), 1)


def sublanes():
    return lax.broadcasted_iota(jnp.int32, (8, 128), 0)


def roll(x, shift):
    shift = shift % 128
    return x if shift == 0 else pltpu.roll(x, shift, 1)


def up(x):
    return pltpu.roll(x, 7, 0)


def down(x):
    return pltpu.roll(x, 1, 0)


def strided(halves, lead, t, half, stride):
    return halves[half][(*lead, pl.ds(t, 8, stride=stride), slice(None))]


def half_specs(*leads):
    return [
        pl.BlockSpec((*lead, SIDE, 128), lambda i, n=len(lead), h=h: (0,) * (n + 1) + (h,))
        for lead in leads
        for h in range(2)
    ]


def doubled(*arrays):
    return [a for a in arrays for _ in range(2)]


def paired(refs):
    return [refs[i : i + 2] for i in range(0, len(refs), 2)]


def planes_at(field, kx, ky, sea, t, half):
    land = strided(sea, (), t, half, ROWS).astype(jnp.float32)
    out = [strided(field, (l,), t, half, ROWS) * land for l in range(LEV)]
    return out + [land, strided(kx, (), t, half, ROWS), strided(ky, (), t, half, ROWS)]


def pack_kernel(links, *refs):
    field, kx, ky, sea = paired(refs[:8])
    west, east, north, nw, ne, rows = refs[8:]
    lane = lanes()
    group = lane // 16
    for t in range(ROWS):
        low = planes_at(field, kx, ky, sea, t, 0)
        high = planes_at(field, kx, ky, sea, t, 1)
        w, e = low[0], roll(high[0], 16)
        for p in range(1, PLANES):
            w = jnp.where(group == SLOT[p], roll(low[p], 16 * SLOT[p]), w)
            e = jnp.where(group == SLOT[p], roll(high[p], 16 * SLOT[p] + 16), e)
        west[8 * t : 8 * t + 8, :] = w
        east[8 * t : 8 * t + 8, :] = e
    flip = 127 - lane
    for p in range(PLANES):
        for o in range(2):
            for half in range(2):
                at = pl.ds(SIDE - 16 + 8 * o, 8)
                if p <= LEV:
                    x = sea[half][at, :].astype(jnp.float32)
                    x = field[half][p, at, :] * x if p < LEV else x
                else:
                    x = (kx, ky)[p - LEV - 1][half][at, :]
                x = jnp.take_along_axis(x, flip, axis=1)
                rows[p, 8 * o : 8 * o + 8, 128 * (1 - half) : 128 * (1 - half) + 128] = x
    for k in range(16):
        north[:, k, :] = rows[:, 15 - k, :]
    west_open = jnp.where(links[0, 0] >= 0, 1.0, 0.0).astype(jnp.float32)
    east_open = jnp.where(links[0, 1] >= 0, 1.0, 0.0).astype(jnp.float32)
    north[LEV, 14, :] = jnp.full((SIDE,), 1.0, jnp.float32) * west_open
    north[LEV, 15, :] = jnp.full((SIDE,), 1.0, jnp.float32) * east_open
    swap = jnp.bitwise_xor(lane, 15)
    for k in range(16):
        r = 8 * (ROWS - 1 - k) + 7
        nw[k : k + 1, :] = west[r : r + 1, :]
        ne[k : k + 1, :] = east[r : r + 1, :]
    for o in range(2):
        nw[8 * o : 8 * o + 8, :] = jnp.take_along_axis(nw[8 * o : 8 * o + 8, :], swap, axis=1)
        ne[8 * o : 8 * o + 8, :] = jnp.take_along_axis(ne[8 * o : 8 * o + 8, :], swap, axis=1)


def pack(links, field, kx, ky, sea):
    f32 = jnp.float32
    shapes = [(SIDE, 128), (SIDE, 128), (PLANES, 16, SIDE), (16, 128), (16, 128)]
    return pl.pallas_call(
        pack_kernel,
        out_shape=[jax.ShapeDtypeStruct(s, f32) for s in shapes],
        grid=(1,),
        in_specs=[SMEM] + half_specs((LEV,), (), (), ()),
        out_specs=[VMEM] * 5,
        scratch_shapes=[pltpu.VMEM((PLANES, 16, SIDE), f32)],
        compiler_params=pltpu.CompilerParams(vmem_limit_bytes=60 << 20),
        name="pack",
    )(links, *doubled(field, kx, ky, sea))


EVEN, ODD = slice(0, 128), slice(128, 256)
HALVES = (EVEN, ODD)


def sorter():
    col = lax.broadcasted_iota(jnp.int32, (SIDE, SIDE), 0)
    at = lax.broadcasted_iota(jnp.int32, (SIDE, SIDE), 1)
    want = jnp.where(at < 128, 2 * at, 2 * at - 255)
    return (col == want).astype(jnp.float32).astype(jnp.bfloat16)


def sort_columns(x, right):
    big = x.astype(jnp.bfloat16)
    small = (x - big.astype(jnp.float32)).astype(jnp.bfloat16)
    return jnp.dot(big, right, preferred_element_type=jnp.float32) + jnp.dot(
        small, right, preferred_element_type=jnp.float32
    )


def wide_weights(sea, kx, ky, rows, we, ww, wn):
    lane, sub = lanes(), sublanes()
    for t in range(rows):
        s = [sea(t, h) for h in range(2)]
        x = [kx(t, h) for h in range(2)]
        we[t, :, EVEN] = 0.5 * (x[0] + x[1]) * s[0] * s[1]
        w = 0.5 * (x[1] + roll(x[0], -1)) * s[1] * roll(s[0], -1)
        w = jnp.where(lane == 127, 0.0, w)
        we[t, :, ODD] = w
        ww[t] = roll(w, 1)
        for h in range(2):
            if t < rows - 1:
                sn, yn = sea(t + 1, h), ky(t + 1, h)
            else:
                sn, yn = up(sea(0, h)), up(ky(0, h))
            w = 0.5 * (ky(t, h) + yn) * s[h] * sn
            if t == rows - 1:
                w = jnp.where(sub == 7, 0.0, w)
            wn[t, :, HALVES[h]] = w


def wide_step(src, dst, we, ww, wn, rows, levels):
    below = []
    for l in levels:
        for h in HALVES:
            over = up(src[l, 0, :, h])
            src[l, rows, :, h] = over
            below.append(down(wn[rows - 1, :, h] * (over - src[l, rows - 1, :, h])))
    here = [src[l, 0, :, h] for l in levels for h in HALVES]
    for t in range(rows):
        e = [we[t, :, h] for h in HALVES]
        n = [wn[t, :, h] for h in HALVES]
        w = ww[t]
        nxt = [src[l, t + 1, :, h] for l in levels for h in HALVES]
        flux = [n[i % 2] * (nxt[i] - here[i]) for i in range(len(here))]
        for i, l in zip(range(0, len(here), 2), levels):
            a, b = here[i : i + 2]
            f = e[0] * (b - a)
            dst[l, t, :, EVEN] = (a + f) + w * (roll(b, 1) - a) + (flux[i] - below[i])
            dst[l, t, :, ODD] = (b - f) + e[1] * (roll(a, -1) - b) + (flux[i + 1] - below[i + 1])
        here, below = nxt, flux


def mixing(vertical):
    levels = vertical.shape[0]
    size = 16 * levels

    def at(shape, axis):
        return lax.broadcasted_iota(jnp.int32, shape, axis)

    left = (at((size, levels), 0) // 16 == at((size, levels), 1)).astype(jnp.float32).astype(jnp.bfloat16)
    right = (at((levels, size), 1) // 16 == at((levels, size), 0)).astype(jnp.float32).astype(jnp.bfloat16)
    tall = jnp.dot(left, vertical, preferred_element_type=jnp.float32).astype(jnp.bfloat16)
    full = jnp.dot(tall, right, preferred_element_type=jnp.float32)
    same = at((size, size), 0) % 16 == at((size, size), 1) % 16
    return jnp.where(same, full, 0.0).astype(jnp.bfloat16)


def own_tile(low, high, i):
    group = lanes() // 32
    a, b = TILES[i]
    x = jnp.where(group == 0, roll(low[a], HALO), roll(high[a], 32 - 108))
    y = jnp.where(group == 2, roll(low[b], 64 + HALO), roll(high[b], 96 - 108))
    return jnp.where(group < 2, x, y)


def inner_kernel(*refs):
    field, kx, ky, sea = paired(refs[:8])
    vertical, cur, own, top, mixer, other, raw, st, we, ww, wn = refs[8:]
    for t in range(ROWS):
        low = planes_at(field, kx, ky, sea, t, 0)
        high = planes_at(field, kx, ky, sea, t, 1)
        for p in range(PLANES):
            raw[p, t, :, 0:128] = low[p]
            raw[p, t, :, 128:256] = high[p]
        for i in range(4):
            own[i, t] = own_tile(low, high, i)
    right = sorter()
    for p in range(PLANES):
        x = sort_columns(raw[p].reshape(SIDE, SIDE), right).reshape(ROWS, 8, SIDE)
        if p < LEV:
            cur[p, 0:ROWS] = x
        else:
            st[p - LEV] = x

    def plane(p):
        return lambda t, h: st[p, t, :, HALVES[h]]

    wide_weights(plane(0), plane(1), plane(2), ROWS, we, ww, wn)
    for h in range(2):
        cols = slice(128 * h, 128 * h + 128)
        land = sea[h][SIDE - TOP :, :].astype(jnp.float32)
        for l in range(LEV):
            top[l, :, cols] = field[h][l, SIDE - TOP :, :] * land
        top[LEV, :, cols] = land
        top[LEV + 1, :, cols] = kx[h][SIDE - TOP :, :]
        top[LEV + 2, :, cols] = ky[h][SIDE - TOP :, :]
    mixer[...] = mixing(vertical[...])

    def two_steps(_, none):
        wide_step(cur, other, we, ww, wn, ROWS, range(LEV))
        wide_step(other, cur, we, ww, wn, ROWS, range(LEV))
        return none

    lax.fori_loop(0, STEPS // 2, two_steps, 0)


def inner(field, kx, ky, sea, vertical):
    f32 = jnp.float32
    scratch = [
        (LEV, ROWS + 1, 8, SIDE),
        (PLANES, ROWS, 8, SIDE),
        (3, ROWS, 8, SIDE),
        (ROWS, 8, SIDE),
        (ROWS, 8, 128),
        (ROWS, 8, SIDE),
    ]
    shapes = [(LEV, ROWS + 1, 8, SIDE), (4, ROWS, 8, 128), (PLANES, TOP, SIDE)]
    return pl.pallas_call(
        inner_kernel,
        out_shape=[jax.ShapeDtypeStruct(s, f32) for s in shapes] + [jax.ShapeDtypeStruct((640, 640), jnp.bfloat16)],
        grid=(1,),
        in_specs=half_specs((LEV,), (), (), ()) + [VMEM],
        out_specs=[VMEM] * 4,
        scratch_shapes=[pltpu.VMEM(s, f32) for s in scratch],
        compiler_params=pltpu.CompilerParams(vmem_limit_bytes=24 << 20),
        cost_estimate=pl.CostEstimate(flops=40_000_000, bytes_accessed=40_000_000, transcendentals=0),
        name="inner",
    )(*doubled(field, kx, ky, sea), vertical)


def strip_step(src, dst, we, ww, wn, tiles):
    sub = sublanes()
    below = []
    for k in tiles:
        over = jnp.where(sub == 7, src[k, ROWS], up(src[k, 0]))
        src[k, ROWS] = over
        below.append(jnp.where(sub == 0, 0.0, down(wn[ROWS - 1] * (over - src[k, ROWS - 1]))))
    here = [src[k, 0] for k in tiles]
    for t in range(STRIP):
        e, w, n = we[t], ww[t], wn[t]
        nxt = [src[k, t + 1] for k in tiles]
        flux = [n * (x - c) for x, c in zip(nxt, here)]
        for k, c, f, g in zip(tiles, here, flux, below):
            dst[k, t] = c + e * (roll(c, -1) - c) + w * (roll(c, 1) - c) + (f - g)
        here, below = nxt, flux


def rim_kernel(links, inside, own, top, west, east, north, nw, ne, out, cur, other, we, ww, wn, kap, sea, ext, nbr, nb_even, nb_odd, nc, n_other, nwe, nww, nwn):
    lane, sub = lanes(), sublanes()
    group, part = lane // 32, lane % 32
    w_halo = (part < HALO) & (group % 2 == 0)
    e_halo = (part >= 20) & (group % 2 == 1)
    ones = jnp.ones((8, 128), jnp.float32)

    def with_halo(i, mine, w, e):
        x = jnp.where(w_halo, roll(w, W_SHIFT[i]), mine)
        return jnp.where(e_halo, roll(e, E_SHIFT[i]), x)

    strips = (cur.at[0], cur.at[1], cur.at[2], kap)
    for t in range(ROWS):
        w, e = west[8 * t : 8 * t + 8, :], east[8 * t : 8 * t + 8, :]
        for i in range(4):
            strips[i][t] = with_halo(i, own[i, t], w, e)
    for o in range(2):
        rows = slice(8 * o, 8 * o + 8)
        low = [north[p, rows, 0:128] for p in range(PLANES)]
        high = [north[p, rows, 128:256] for p in range(PLANES)]
        for i in range(4):
            ext[i, rows, :] = with_halo(i, own_tile(low, high, i), nw[rows, :], ne[rows, :])
    for k in range(DEPTH):
        for i in range(4):
            strips[i][ROWS + k] = jnp.broadcast_to(ext[i, k : k + 1, :], (8, 128))

    def flag(x):
        return jnp.where(x >= 0, 1.0, 0.0).astype(jnp.float32)

    w_open = ones * flag(links[0, 0])
    e_open = ones * flag(links[0, 1])
    w_over = jnp.broadcast_to(north[LEV, 15:16, 0:128], (8, 128))
    e_over = jnp.broadcast_to(north[LEV, 14:15, 0:128], (8, 128))
    seams = []
    for a, b in ((w_open, e_open), (w_over, e_over)):
        m = jnp.where(lane == HALO - 1, a, jnp.where(lane == 32 + 19, b, 1.0))
        seams.append(0.5 * jnp.where(part == 31, 0.0, m))
    first = group < 2
    for t in range(STRIP):
        c = cur[2, t]
        sea[t] = jnp.where(first, roll(c, 64), c)
    for t in range(STRIP):
        s, x = sea[t], kap[t]
        w = seams[t >= ROWS] * (x + roll(x, -1)) * s * roll(s, -1)
        w = jnp.where(first, w, roll(w, 64))
        we[t] = w
        ww[t] = roll(w, 1)
        if t < STRIP - 1:
            sn, yn = sea[t + 1], kap[t + 1]
            if t == ROWS - 1:
                sn = jnp.where(sub == 7, sn, up(sea[0]))
                yn = jnp.where(sub == 7, yn, up(kap[0]))
            w = 0.5 * (x + yn) * s * sn
            wn[t] = jnp.where(first, roll(w, 64), w)
    zeros = jnp.zeros((8, 128), jnp.float32)
    wn[STRIP - 1] = zeros
    for i in range(3):
        cur[i, STRIP] = zeros
        other[i, STRIP] = zeros

    nbr[:, 0:TOP, :] = top[...]
    nbr[:, TOP : TOP + 16, :] = north[...]
    x = sort_columns(nbr[...].reshape(PLANES * (TOP + 16), SIDE), sorter()).reshape(PLANES, TOP + 16, SIDE)
    nb = (nb_even, nb_odd)
    for h in range(2):
        nb[h][...] = x[:, :, HALVES[h]]
    for l in range(LEV):
        for t in range(NORTH):
            for h in range(2):
                nc[l, t, :, HALVES[h]] = strided(nb, (l,), t, h, NORTH)

    def plane(p):
        return lambda t, h: strided(nb, (p,), t, h, NORTH)

    wide_weights(plane(LEV), plane(LEV + 1), plane(LEV + 2), NORTH, nwe, nww, nwn)

    def two_steps(_, none):
        strip_step(cur, other, we, ww, wn, range(3))
        wide_step(nc, n_other, nwe, nww, nwn, NORTH, range(LEV))
        strip_step(other, cur, we, ww, wn, range(3))
        wide_step(n_other, nc, nwe, nww, nwn, NORTH, range(LEV))
        return none

    lax.fori_loop(0, STEPS // 2, two_steps, 0)

    for l in range(LEV):
        for t in range(NORTH):
            for h in range(2):
                nb[h][l, pl.ds(t, 8, stride=NORTH), :] = nc[l, t, :, HALVES[h]]

    on_rim = (lane < 5) | (lane >= 123)
    top_row = sub == 7
    for l in range(LEV):
        i, base = l // 2, 64 * (l % 2)
        pick = [
            jnp.where(lane < 5, base + HALO + 2 * lane + h, jnp.where(lane >= 123, base + 42 + 2 * (lane - 123) + h, 0))
            for h in range(2)
        ]
        for t in range(0, ROWS, 2):
            pair = []
            for u in (t, t + 1):
                for h in range(2):
                    x = inside[l, u, :, HALVES[h]]
                    if u >= ROWS - DEPTH:
                        r = TOP - ROWS + u
                        x = jnp.where(top_row, jnp.broadcast_to(nb[h][l, r : r + 1, :], (8, 128)), x)
                    pair.append(jnp.where(on_rim, jnp.take_along_axis(cur[i, u], pick[h], axis=1), x))
            q, r = t // 4, 8 * (t % 4)
            for h in range(2):
                x = jnp.concatenate([pair[h], pair[2 + h]], axis=0)
                out[q, l, r : r + 16, HALVES[h]] = x.astype(jnp.bfloat16)


def rim(links, inside, own, top, west, east, north, nw, ne):
    f32 = jnp.float32
    scratch = [
        (3, STRIP + 1, 8, 128),
        (3, STRIP + 1, 8, 128),
        (STRIP, 8, 128),
        (STRIP, 8, 128),
        (STRIP, 8, 128),
        (STRIP, 8, 128),
        (STRIP, 8, 128),
        (4, 16, 128),
        (PLANES, TOP + 16, SIDE),
        (PLANES, TOP + 16, 128),
        (PLANES, TOP + 16, 128),
        (LEV, NORTH + 1, 8, SIDE),
        (LEV, NORTH + 1, 8, SIDE),
        (NORTH, 8, SIDE),
        (NORTH, 8, 128),
        (NORTH, 8, SIDE),
    ]
    return pl.pallas_call(
        rim_kernel,
        out_shape=jax.ShapeDtypeStruct((CHUNKS, LEV, SIDE // CHUNKS, SIDE), jnp.bfloat16),
        in_specs=[SMEM] + [VMEM] * 8,
        out_specs=VMEM,
        scratch_shapes=[pltpu.VMEM(s, f32) for s in scratch],
        compiler_params=pltpu.CompilerParams(vmem_limit_bytes=24 << 20),
        name="rim",
    )(links, inside, own, top, west, east, north, nw, ne)


def mix_kernel(x, k, y):
    for h in range(2):
        rows = x[:, :, 16 * h : 16 * h + 16, :].reshape(CHUNKS * LEV * 16, SIDE)
        mixed = jnp.dot(k[...], rows, preferred_element_type=jnp.float32).astype(jnp.bfloat16)
        y[:, :, 16 * h : 16 * h + 16, :] = mixed.reshape(CHUNKS, LEV, 16, SIDE)


def mix(x, k):
    return pl.pallas_call(
        mix_kernel,
        out_shape=jax.ShapeDtypeStruct(x.shape, jnp.bfloat16),
        in_specs=[VMEM] * 2,
        out_specs=VMEM,
        compiler_params=pltpu.CompilerParams(vmem_limit_bytes=24 << 20),
        name="mix",
    )(x, k)


def unpack_kernel(z, out):
    at = lax.broadcasted_iota(jnp.int32, (SIDE, 128), 0)
    col = lax.broadcasted_iota(jnp.int32, (SIDE, 128), 1) + 128 * pl.program_id(0)
    back = (jnp.where(at < 128, 2 * at, 2 * at - 255) == col).astype(jnp.float32).astype(jnp.bfloat16)
    for q in range(CHUNKS):
        x = jnp.dot(z[q].reshape(LEV * 32, SIDE), back, preferred_element_type=jnp.float32)
        for l in range(LEV):
            for u in range(4):
                r = 32 * l + 8 * u
                out[l, pl.ds(4 * q + u, 8, stride=ROWS), :] = x[r : r + 8]


def unpack(z):
    return pl.pallas_call(
        unpack_kernel,
        out_shape=jax.ShapeDtypeStruct((LEV, SIDE, SIDE), jnp.float32),
        grid=(2,),
        in_specs=[pl.BlockSpec((CHUNKS, LEV, SIDE // CHUNKS, SIDE), lambda h: (0, 0, 0, 0))],
        out_specs=pl.BlockSpec((LEV, SIDE, 128), lambda h: (0, 0, h)),
        compiler_params=pltpu.CompilerParams(vmem_limit_bytes=24 << 20),
        name="unpack",
    )(z)


def shards(field, kappa_x, kappa_y, sea_mask, tile_links, vertical):
    tiles = lax.axis_size("tile")

    def send(x, target):
        return lax.ppermute(x, "tile", [(i, target(i) % tiles) for i in range(tiles)])

    cells, kx, ky, sea = field[0], kappa_x[0], kappa_y[0], sea_mask[0]
    west, east, north, nw, ne = pack(tile_links, cells, kx, ky, sea)
    from_east = send(west, lambda i: i - 1)
    from_west = send(east, lambda i: i + 1)
    from_north = send(north, lambda i: -i)
    from_nw = send(nw, lambda i: 1 - i)
    from_ne = send(ne, lambda i: -1 - i)
    inside, own, top, mixer = inner(cells, kx, ky, sea, vertical)
    smooth = rim(tile_links, inside, own, top, from_west, from_east, from_north, from_nw, from_ne)
    gathered = lax.all_to_all(smooth, "lev", 0, 0, tiled=True)
    back = lax.all_to_all(mix(gathered, mixer), "lev", 0, 0, tiled=True)
    return unpack(back)[None]


def solution(mesh):
    placed = (
        P("tile", "lev", None, None),
        P("tile", None, None),
        P("tile", None, None),
        P("tile", None, None),
        P("tile", None),
        P(),
    )
    return jax.shard_map(
        shards, mesh=mesh, in_specs=placed, out_specs=P("tile", "lev", None, None), check_vma=False
    )
```

```python
import jax
import jax.numpy as jnp
from jax import lax
from jax.experimental import pallas as pl
from jax.experimental.pallas import tpu as pltpu
from jax.sharding import PartitionSpec as P

STEPS = 10
LEV = 5
PLANES = LEV + 3
SIDE = 256
ROWS = 32
HALO = 12
DEPTH = 10
STRIP = ROWS + DEPTH
TOP = 24
NORTH = 5
CHUNKS = 8
SLOT = (0, 4, 2, 6, 1, 5, 3, 7)
TILES = ((0, 1), (2, 3), (4, 5), (6, 7))
W_SHIFT = (-4, -36, -20, -52)
E_SHIFT = (52, 20, 36, 4)

VMEM = pl.BlockSpec(memory_space=pltpu.VMEM)
SMEM = pl.BlockSpec(memory_space=pltpu.SMEM)


def lanes():
    return lax.broadcasted_iota(jnp.int32, (8, 128), 1)


def sublanes():
    return lax.broadcasted_iota(jnp.int32, (8, 128), 0)


def roll(x, shift):
    shift = shift % 128
    return x if shift == 0 else pltpu.roll(x, shift, 1)


def up(x):
    return pltpu.roll(x, 7, 0)


def down(x):
    return pltpu.roll(x, 1, 0)


def strided(halves, lead, t, half, stride):
    return halves[half][(*lead, pl.ds(t, 8, stride=stride), slice(None))]


def half_specs(*leads):
    return [
        pl.BlockSpec((*lead, SIDE, 128), lambda i, n=len(lead), h=h: (0,) * (n + 1) + (h,))
        for lead in leads
        for h in range(2)
    ]


def doubled(*arrays):
    return [a for a in arrays for _ in range(2)]


def paired(refs):
    return [refs[i : i + 2] for i in range(0, len(refs), 2)]


def planes_at(field, kx, ky, sea, t, half):
    land = strided(sea, (), t, half, ROWS).astype(jnp.float32)
    out = [strided(field, (l,), t, half, ROWS) * land for l in range(LEV)]
    return out + [land, strided(kx, (), t, half, ROWS), strided(ky, (), t, half, ROWS)]


def pack_kernel(links, *refs):
    field, kx, ky, sea = paired(refs[:8])
    west, east, north, nw, ne, rows = refs[8:]
    lane = lanes()
    group = lane // 16
    for t in range(ROWS):
        low = planes_at(field, kx, ky, sea, t, 0)
        high = planes_at(field, kx, ky, sea, t, 1)
        w, e = low[0], roll(high[0], 16)
        for p in range(1, PLANES):
            w = jnp.where(group == SLOT[p], roll(low[p], 16 * SLOT[p]), w)
            e = jnp.where(group == SLOT[p], roll(high[p], 16 * SLOT[p] + 16), e)
        west[8 * t : 8 * t + 8, :] = w
        east[8 * t : 8 * t + 8, :] = e
    flip = 127 - lane
    for p in range(PLANES):
        for o in range(2):
            for half in range(2):
                at = pl.ds(SIDE - 16 + 8 * o, 8)
                if p <= LEV:
                    x = sea[half][at, :].astype(jnp.float32)
                    x = field[half][p, at, :] * x if p < LEV else x
                else:
                    x = (kx, ky)[p - LEV - 1][half][at, :]
                x = jnp.take_along_axis(x, flip, axis=1)
                rows[p, 8 * o : 8 * o + 8, 128 * (1 - half) : 128 * (1 - half) + 128] = x
    for k in range(16):
        north[:, k, :] = rows[:, 15 - k, :]
    west_open = jnp.where(links[0, 0] >= 0, 1.0, 0.0).astype(jnp.float32)
    east_open = jnp.where(links[0, 1] >= 0, 1.0, 0.0).astype(jnp.float32)
    north[LEV, 14, :] = jnp.full((SIDE,), 1.0, jnp.float32) * west_open
    north[LEV, 15, :] = jnp.full((SIDE,), 1.0, jnp.float32) * east_open
    swap = jnp.bitwise_xor(lane, 15)
    for k in range(16):
        r = 8 * (ROWS - 1 - k) + 7
        nw[k : k + 1, :] = west[r : r + 1, :]
        ne[k : k + 1, :] = east[r : r + 1, :]
    for o in range(2):
        nw[8 * o : 8 * o + 8, :] = jnp.take_along_axis(nw[8 * o : 8 * o + 8, :], swap, axis=1)
        ne[8 * o : 8 * o + 8, :] = jnp.take_along_axis(ne[8 * o : 8 * o + 8, :], swap, axis=1)


def pack(links, field, kx, ky, sea):
    f32 = jnp.float32
    shapes = [(SIDE, 128), (SIDE, 128), (PLANES, 16, SIDE), (16, 128), (16, 128)]
    return pl.pallas_call(
        pack_kernel,
        out_shape=[jax.ShapeDtypeStruct(s, f32) for s in shapes],
        grid=(1,),
        in_specs=[SMEM] + half_specs((LEV,), (), (), ()),
        out_specs=[VMEM] * 5,
        scratch_shapes=[pltpu.VMEM((PLANES, 16, SIDE), f32)],
        compiler_params=pltpu.CompilerParams(vmem_limit_bytes=60 << 20),
        name="pack",
    )(links, *doubled(field, kx, ky, sea))


EVEN, ODD = slice(0, 128), slice(128, 256)
HALVES = (EVEN, ODD)


def sorter():
    col = lax.broadcasted_iota(jnp.int32, (SIDE, SIDE), 0)
    at = lax.broadcasted_iota(jnp.int32, (SIDE, SIDE), 1)
    want = jnp.where(at < 128, 2 * at, 2 * at - 255)
    return (col == want).astype(jnp.float32).astype(jnp.bfloat16)


def sort_columns(x, right):
    big = x.astype(jnp.bfloat16)
    small = (x - big.astype(jnp.float32)).astype(jnp.bfloat16)
    return jnp.dot(big, right, preferred_element_type=jnp.float32) + jnp.dot(
        small, right, preferred_element_type=jnp.float32
    )


def wide_weights(sea, kx, ky, rows, we, ww, wn):
    lane, sub = lanes(), sublanes()
    for t in range(rows):
        s = [sea(t, h) for h in range(2)]
        x = [kx(t, h) for h in range(2)]
        we[t, :, EVEN] = 0.5 * (x[0] + x[1]) * s[0] * s[1]
        w = 0.5 * (x[1] + roll(x[0], -1)) * s[1] * roll(s[0], -1)
        w = jnp.where(lane == 127, 0.0, w)
        we[t, :, ODD] = w
        ww[t] = roll(w, 1)
        for h in range(2):
            if t < rows - 1:
                sn, yn = sea(t + 1, h), ky(t + 1, h)
            else:
                sn, yn = up(sea(0, h)), up(ky(0, h))
            w = 0.5 * (ky(t, h) + yn) * s[h] * sn
            if t == rows - 1:
                w = jnp.where(sub == 7, 0.0, w)
            wn[t, :, HALVES[h]] = w


def wide_step(src, dst, we, ww, wn, rows, levels):
    below = []
    for l in levels:
        for h in HALVES:
            over = up(src[l, 0, :, h])
            src[l, rows, :, h] = over
            below.append(down(wn[rows - 1, :, h] * (over - src[l, rows - 1, :, h])))
    here = [src[l, 0, :, h] for l in levels for h in HALVES]
    for t in range(rows):
        e = [we[t, :, h] for h in HALVES]
        n = [wn[t, :, h] for h in HALVES]
        w = ww[t]
        nxt = [src[l, t + 1, :, h] for l in levels for h in HALVES]
        flux = [n[i % 2] * (nxt[i] - here[i]) for i in range(len(here))]
        for i, l in zip(range(0, len(here), 2), levels):
            a, b = here[i : i + 2]
            f = e[0] * (b - a)
            dst[l, t, :, EVEN] = (a + f) + w * (roll(b, 1) - a) + (flux[i] - below[i])
            dst[l, t, :, ODD] = (b - f) + e[1] * (roll(a, -1) - b) + (flux[i + 1] - below[i + 1])
        here, below = nxt, flux


def mixing(vertical):
    levels = vertical.shape[0]
    size = 16 * levels

    def at(shape, axis):
        return lax.broadcasted_iota(jnp.int32, shape, axis)

    left = (at((size, levels), 0) // 16 == at((size, levels), 1)).astype(jnp.float32).astype(jnp.bfloat16)
    right = (at((levels, size), 1) // 16 == at((levels, size), 0)).astype(jnp.float32).astype(jnp.bfloat16)
    tall = jnp.dot(left, vertical, preferred_element_type=jnp.float32).astype(jnp.bfloat16)
    full = jnp.dot(tall, right, preferred_element_type=jnp.float32)
    same = at((size, size), 0) % 16 == at((size, size), 1) % 16
    return jnp.where(same, full, 0.0).astype(jnp.bfloat16)


def own_tile(low, high, i):
    group = lanes() // 32
    a, b = TILES[i]
    x = jnp.where(group == 0, roll(low[a], HALO), roll(high[a], 32 - 108))
    y = jnp.where(group == 2, roll(low[b], 64 + HALO), roll(high[b], 96 - 108))
    return jnp.where(group < 2, x, y)


def inner_kernel(*refs):
    field, kx, ky, sea = paired(refs[:8])
    vertical, cur, own, top, mixer, other, raw, st, we, ww, wn = refs[8:]
    for t in range(ROWS):
        low = planes_at(field, kx, ky, sea, t, 0)
        high = planes_at(field, kx, ky, sea, t, 1)
        for p in range(PLANES):
            raw[p, t, :, 0:128] = low[p]
            raw[p, t, :, 128:256] = high[p]
        for i in range(4):
            own[i, t] = own_tile(low, high, i)
    right = sorter()
    for p in range(PLANES):
        x = sort_columns(raw[p].reshape(SIDE, SIDE), right).reshape(ROWS, 8, SIDE)
        if p < LEV:
            cur[p, 0:ROWS] = x
        else:
            st[p - LEV] = x

    def plane(p):
        return lambda t, h: st[p, t, :, HALVES[h]]

    wide_weights(plane(0), plane(1), plane(2), ROWS, we, ww, wn)
    for h in range(2):
        cols = slice(128 * h, 128 * h + 128)
        land = sea[h][SIDE - TOP :, :].astype(jnp.float32)
        for l in range(LEV):
            top[l, :, cols] = field[h][l, SIDE - TOP :, :] * land
        top[LEV, :, cols] = land
        top[LEV + 1, :, cols] = kx[h][SIDE - TOP :, :]
        top[LEV + 2, :, cols] = ky[h][SIDE - TOP :, :]
    mixer[...] = mixing(vertical[...])

    def two_steps(_, none):
        wide_step(cur, other, we, ww, wn, ROWS, range(LEV))
        wide_step(other, cur, we, ww, wn, ROWS, range(LEV))
        return none

    lax.fori_loop(0, STEPS // 2, two_steps, 0)


def inner(field, kx, ky, sea, vertical):
    f32 = jnp.float32
    scratch = [
        (LEV, ROWS + 1, 8, SIDE),
        (PLANES, ROWS, 8, SIDE),
        (3, ROWS, 8, SIDE),
        (ROWS, 8, SIDE),
        (ROWS, 8, 128),
        (ROWS, 8, SIDE),
    ]
    shapes = [(LEV, ROWS + 1, 8, SIDE), (4, ROWS, 8, 128), (PLANES, TOP, SIDE)]
    return pl.pallas_call(
        inner_kernel,
        out_shape=[jax.ShapeDtypeStruct(s, f32) for s in shapes] + [jax.ShapeDtypeStruct((640, 640), jnp.bfloat16)],
        grid=(1,),
        in_specs=half_specs((LEV,), (), (), ()) + [VMEM],
        out_specs=[VMEM] * 4,
        scratch_shapes=[pltpu.VMEM(s, f32) for s in scratch],
        compiler_params=pltpu.CompilerParams(vmem_limit_bytes=24 << 20),
        cost_estimate=pl.CostEstimate(flops=40_000_000, bytes_accessed=40_000_000, transcendentals=0),
        name="inner",
    )(*doubled(field, kx, ky, sea), vertical)


def strip_step(src, dst, we, ww, wn, tiles):
    sub = sublanes()
    below = []
    for k in tiles:
        over = jnp.where(sub == 7, src[k, ROWS], up(src[k, 0]))
        src[k, ROWS] = over
        below.append(jnp.where(sub == 0, 0.0, down(wn[ROWS - 1] * (over - src[k, ROWS - 1]))))
    here = [src[k, 0] for k in tiles]
    for t in range(STRIP):
        e, w, n = we[t], ww[t], wn[t]
        nxt = [src[k, t + 1] for k in tiles]
        flux = [n * (x - c) for x, c in zip(nxt, here)]
        for k, c, f, g in zip(tiles, here, flux, below):
            dst[k, t] = c + e * (roll(c, -1) - c) + w * (roll(c, 1) - c) + (f - g)
        here, below = nxt, flux


def rim_kernel(links, inside, own, top, west, east, north, nw, ne, out, cur, other, we, ww, wn, kap, sea, ext, nbr, nb_even, nb_odd, nc, n_other, nwe, nww, nwn):
    lane, sub = lanes(), sublanes()
    group, part = lane // 32, lane % 32
    w_halo = (part < HALO) & (group % 2 == 0)
    e_halo = (part >= 20) & (group % 2 == 1)
    ones = jnp.ones((8, 128), jnp.float32)

    def with_halo(i, mine, w, e):
        x = jnp.where(w_halo, roll(w, W_SHIFT[i]), mine)
        return jnp.where(e_halo, roll(e, E_SHIFT[i]), x)

    strips = (cur.at[0], cur.at[1], cur.at[2], kap)
    def fill(b, none):
        for j in range(8):
            t = 8 * b + j
            at = pl.ds(pl.multiple_of(8 * t, 8), 8)
            w, e = west[at, :], east[at, :]
            for i in range(4):
                strips[i][t] = with_halo(i, own[i, t], w, e)
        return none

    lax.fori_loop(0, ROWS // 8, fill, 0)
    for o in range(2):
        rows = slice(8 * o, 8 * o + 8)
        low = [north[p, rows, 0:128] for p in range(PLANES)]
        high = [north[p, rows, 128:256] for p in range(PLANES)]
        for i in range(4):
            ext[i, rows, :] = with_halo(i, own_tile(low, high, i), nw[rows, :], ne[rows, :])
    for k in range(DEPTH):
        for i in range(4):
            strips[i][ROWS + k] = jnp.broadcast_to(ext[i, k : k + 1, :], (8, 128))

    def flag(x):
        return jnp.where(x >= 0, 1.0, 0.0).astype(jnp.float32)

    w_open = ones * flag(links[0, 0])
    e_open = ones * flag(links[0, 1])
    w_over = jnp.broadcast_to(north[LEV, 15:16, 0:128], (8, 128))
    e_over = jnp.broadcast_to(north[LEV, 14:15, 0:128], (8, 128))
    seams = []
    for a, b in ((w_open, e_open), (w_over, e_over)):
        m = jnp.where(lane == HALO - 1, a, jnp.where(lane == 32 + 19, b, 1.0))
        seams.append(0.5 * jnp.where(part == 31, 0.0, m))
    first = group < 2
    def spread_sea(b, none):
        for j in range(14):
            c = cur[2, 14 * b + j]
            sea[14 * b + j] = jnp.where(first, roll(c, 64), c)
        return none

    lax.fori_loop(0, STRIP // 14, spread_sea, 0)

    def weights(t, seam, s, x, sn, yn):
        w = seam * (x + roll(x, -1)) * s * roll(s, -1)
        w = jnp.where(first, w, roll(w, 64))
        we[t] = w
        ww[t] = roll(w, 1)
        w = 0.5 * (x + yn) * s * sn
        wn[t] = jnp.where(first, roll(w, 64), w)

    def most_weights(b, none):
        for j in range(14):
            t = 14 * b + j
            weights(t, seams[0], sea[t], kap[t], sea[t + 1], kap[t + 1])
        return none

    lax.fori_loop(0, 2, most_weights, 0)
    for t in range(28, STRIP):
        s, x = sea[t], kap[t]
        sn, yn = (sea[t + 1], kap[t + 1]) if t < STRIP - 1 else (s, x)
        if t == ROWS - 1:
            sn = jnp.where(sub == 7, sn, up(sea[0]))
            yn = jnp.where(sub == 7, yn, up(kap[0]))
        weights(t, seams[t >= ROWS], s, x, sn, yn)
    zeros = jnp.zeros((8, 128), jnp.float32)
    wn[STRIP - 1] = zeros
    for i in range(3):
        cur[i, STRIP] = zeros
        other[i, STRIP] = zeros

    nbr[:, 0:TOP, :] = top[...]
    nbr[:, TOP : TOP + 16, :] = north[...]
    x = sort_columns(nbr[...].reshape(PLANES * (TOP + 16), SIDE), sorter()).reshape(PLANES, TOP + 16, SIDE)
    nb = (nb_even, nb_odd)
    for h in range(2):
        nb[h][...] = x[:, :, HALVES[h]]
    for l in range(LEV):
        for t in range(NORTH):
            for h in range(2):
                nc[l, t, :, HALVES[h]] = strided(nb, (l,), t, h, NORTH)

    def plane(p):
        return lambda t, h: strided(nb, (p,), t, h, NORTH)

    wide_weights(plane(LEV), plane(LEV + 1), plane(LEV + 2), NORTH, nwe, nww, nwn)

    def two_steps(_, none):
        strip_step(cur, other, we, ww, wn, range(3))
        wide_step(nc, n_other, nwe, nww, nwn, NORTH, range(LEV))
        strip_step(other, cur, we, ww, wn, range(3))
        wide_step(n_other, nc, nwe, nww, nwn, NORTH, range(LEV))
        return none

    lax.fori_loop(0, STEPS // 2, two_steps, 0)

    for l in range(LEV):
        for t in range(NORTH):
            for h in range(2):
                nb[h][l, pl.ds(t, 8, stride=NORTH), :] = nc[l, t, :, HALVES[h]]

    on_rim = (lane < 5) | (lane >= 123)
    top_row = sub == 7
    for l in range(LEV):
        i, base = l // 2, 64 * (l % 2)
        pick = [
            jnp.where(lane < 5, base + HALO + 2 * lane + h, jnp.where(lane >= 123, base + 42 + 2 * (lane - 123) + h, 0))
            for h in range(2)
        ]
        for t in range(0, ROWS, 2):
            pair = []
            for u in (t, t + 1):
                for h in range(2):
                    x = inside[l, u, :, HALVES[h]]
                    if u >= ROWS - DEPTH:
                        r = TOP - ROWS + u
                        x = jnp.where(top_row, jnp.broadcast_to(nb[h][l, r : r + 1, :], (8, 128)), x)
                    pair.append(jnp.where(on_rim, jnp.take_along_axis(cur[i, u], pick[h], axis=1), x))
            q, r = t // 4, 8 * (t % 4)
            for h in range(2):
                x = jnp.concatenate([pair[h], pair[2 + h]], axis=0)
                out[q, l, r : r + 16, HALVES[h]] = x.astype(jnp.bfloat16)


def rim(links, inside, own, top, west, east, north, nw, ne):
    f32 = jnp.float32
    scratch = [
        (3, STRIP + 1, 8, 128),
        (3, STRIP + 1, 8, 128),
        (STRIP, 8, 128),
        (STRIP, 8, 128),
        (STRIP, 8, 128),
        (STRIP, 8, 128),
        (STRIP, 8, 128),
        (4, 16, 128),
        (PLANES, TOP + 16, SIDE),
        (PLANES, TOP + 16, 128),
        (PLANES, TOP + 16, 128),
        (LEV, NORTH + 1, 8, SIDE),
        (LEV, NORTH + 1, 8, SIDE),
        (NORTH, 8, SIDE),
        (NORTH, 8, 128),
        (NORTH, 8, SIDE),
    ]
    return pl.pallas_call(
        rim_kernel,
        out_shape=jax.ShapeDtypeStruct((CHUNKS, LEV, SIDE // CHUNKS, SIDE), jnp.bfloat16),
        in_specs=[SMEM] + [VMEM] * 8,
        out_specs=VMEM,
        scratch_shapes=[pltpu.VMEM(s, f32) for s in scratch],
        compiler_params=pltpu.CompilerParams(vmem_limit_bytes=24 << 20),
        name="rim",
    )(links, inside, own, top, west, east, north, nw, ne)


def mix_kernel(x, k, y):
    for h in range(2):
        rows = x[:, :, 16 * h : 16 * h + 16, :].reshape(CHUNKS * LEV * 16, SIDE)
        mixed = jnp.dot(k[...], rows, preferred_element_type=jnp.float32).astype(jnp.bfloat16)
        y[:, :, 16 * h : 16 * h + 16, :] = mixed.reshape(CHUNKS, LEV, 16, SIDE)


def mix(x, k):
    return pl.pallas_call(
        mix_kernel,
        out_shape=jax.ShapeDtypeStruct(x.shape, jnp.bfloat16),
        in_specs=[VMEM] * 2,
        out_specs=VMEM,
        compiler_params=pltpu.CompilerParams(vmem_limit_bytes=24 << 20),
        name="mix",
    )(x, k)


def unpack_kernel(z, out):
    at = lax.broadcasted_iota(jnp.int32, (SIDE, 128), 0)
    col = lax.broadcasted_iota(jnp.int32, (SIDE, 128), 1) + 128 * pl.program_id(0)
    back = (jnp.where(at < 128, 2 * at, 2 * at - 255) == col).astype(jnp.float32).astype(jnp.bfloat16)
    for q in range(CHUNKS):
        x = jnp.dot(z[q].reshape(LEV * 32, SIDE), back, preferred_element_type=jnp.float32)
        for l in range(LEV):
            for u in range(4):
                r = 32 * l + 8 * u
                out[l, pl.ds(4 * q + u, 8, stride=ROWS), :] = x[r : r + 8]


def unpack(z):
    return pl.pallas_call(
        unpack_kernel,
        out_shape=jax.ShapeDtypeStruct((LEV, SIDE, SIDE), jnp.float32),
        grid=(2,),
        in_specs=[pl.BlockSpec((CHUNKS, LEV, SIDE // CHUNKS, SIDE), lambda h: (0, 0, 0, 0))],
        out_specs=pl.BlockSpec((LEV, SIDE, 128), lambda h: (0, 0, h)),
        compiler_params=pltpu.CompilerParams(vmem_limit_bytes=24 << 20),
        name="unpack",
    )(z)


def shards(field, kappa_x, kappa_y, sea_mask, tile_links, vertical):
    tiles = lax.axis_size("tile")

    def send(x, target):
        return lax.ppermute(x, "tile", [(i, target(i) % tiles) for i in range(tiles)])

    cells, kx, ky, sea = field[0], kappa_x[0], kappa_y[0], sea_mask[0]
    west, east, north, nw, ne = pack(tile_links, cells, kx, ky, sea)
    from_east = send(west, lambda i: i - 1)
    from_west = send(east, lambda i: i + 1)
    from_north = send(north, lambda i: -i)
    from_nw = send(nw, lambda i: 1 - i)
    from_ne = send(ne, lambda i: -1 - i)
    inside, own, top, mixer = inner(cells, kx, ky, sea, vertical)
    smooth = rim(tile_links, inside, own, top, from_west, from_east, from_north, from_nw, from_ne)
    gathered = lax.all_to_all(smooth, "lev", 0, 0, tiled=True)
    back = lax.all_to_all(mix(gathered, mixer), "lev", 0, 0, tiled=True)
    return unpack(back)[None]


def solution(mesh):
    placed = (
        P("tile", "lev", None, None),
        P("tile", None, None),
        P("tile", None, None),
        P("tile", None, None),
        P("tile", None),
        P(),
    )
    return jax.shard_map(
        shards, mesh=mesh, in_specs=placed, out_specs=P("tile", "lev", None, None), check_vma=False
    )
```

```python
import jax
import jax.numpy as jnp
from jax import lax
from jax.experimental import pallas as pl
from jax.experimental.pallas import tpu as pltpu
from jax.sharding import PartitionSpec as P

STEPS = 10
LEV = 5
PLANES = LEV + 3
SIDE = 256
ROWS = 32
HALO = 12
DEPTH = 10
STRIP = ROWS + DEPTH
TOP = 24
NORTH = 5
CHUNKS = 8
PACK_ROWS = 128
SLOT = (0, 4, 2, 6, 1, 5, 3, 7)
TILES = ((0, 1), (2, 3), (4, 5), (6, 7))
W_SHIFT = (-4, -36, -20, -52)
E_SHIFT = (52, 20, 36, 4)

VMEM = pl.BlockSpec(memory_space=pltpu.VMEM)
SMEM = pl.BlockSpec(memory_space=pltpu.SMEM)


def lanes():
    return lax.broadcasted_iota(jnp.int32, (8, 128), 1)


def sublanes():
    return lax.broadcasted_iota(jnp.int32, (8, 128), 0)


def roll(x, shift):
    shift = shift % 128
    return x if shift == 0 else pltpu.roll(x, shift, 1)


def up(x):
    return pltpu.roll(x, 7, 0)


def down(x):
    return pltpu.roll(x, 1, 0)


def strided(halves, lead, t, half, stride):
    return halves[half][(*lead, pl.ds(t, 8, stride=stride), slice(None))]


def half_specs(*leads):
    return [
        pl.BlockSpec((*lead, SIDE, 128), lambda i, n=len(lead), h=h: (0,) * (n + 1) + (h,))
        for lead in leads
        for h in range(2)
    ]


def doubled(*arrays):
    return [a for a in arrays for _ in range(2)]


def paired(refs):
    return [refs[i : i + 2] for i in range(0, len(refs), 2)]


def planes_at(field, kx, ky, sea, t, half):
    land = strided(sea, (), t, half, ROWS).astype(jnp.float32)
    out = [strided(field, (l,), t, half, ROWS) * land for l in range(LEV)]
    return out + [land, strided(kx, (), t, half, ROWS), strided(ky, (), t, half, ROWS)]


def pack_kernel(links, field, kx, ky, sea, west, east, north, nw, ne, rows):
    lane = lanes()
    group = lane // 16
    start = PACK_ROWS * pl.program_id(0)

    def planes(at, cols):
        land = sea[at, cols].astype(jnp.float32)
        return [field[l, at, cols] * land for l in range(LEV)] + [land, kx[at, cols], ky[at, cols]]

    for t in range(PACK_ROWS // 8):
        at = slice(8 * t, 8 * t + 8)
        low, high = planes(at, slice(0, 128)), planes(at, slice(128, 256))
        w, e = low[0], roll(high[0], 16)
        for p in range(1, PLANES):
            w = jnp.where(group == SLOT[p], roll(low[p], 16 * SLOT[p]), w)
            e = jnp.where(group == SLOT[p], roll(high[p], 16 * SLOT[p] + 16), e)
        to = pl.ds(pl.multiple_of(start + 8 * t, 8), 8)
        west[to, :] = w
        east[to, :] = e

    @pl.when(pl.program_id(0) == SIDE // PACK_ROWS - 1)
    def _():
        pack_top(links, planes, west, east, north, nw, ne, rows)


def pack_top(links, planes, west, east, north, nw, ne, rows):
    lane = lanes()
    flip = 127 - lane
    for o in range(2):
        for half in range(2):
            at = slice(PACK_ROWS - 16 + 8 * o, PACK_ROWS - 8 + 8 * o)
            for p, x in enumerate(planes(at, slice(128 * half, 128 * half + 128))):
                x = jnp.take_along_axis(x, flip, axis=1)
                rows[p, 8 * o : 8 * o + 8, 128 * (1 - half) : 128 * (1 - half) + 128] = x
    for k in range(16):
        north[:, k, :] = rows[:, 15 - k, :]
    west_open = jnp.where(links[0, 0] >= 0, 1.0, 0.0).astype(jnp.float32)
    east_open = jnp.where(links[0, 1] >= 0, 1.0, 0.0).astype(jnp.float32)
    north[LEV, 14, :] = jnp.full((SIDE,), 1.0, jnp.float32) * west_open
    north[LEV, 15, :] = jnp.full((SIDE,), 1.0, jnp.float32) * east_open
    swap = jnp.bitwise_xor(lane, 15)
    for k in range(16):
        r = SIDE - 1 - k
        nw[k : k + 1, :] = west[r : r + 1, :]
        ne[k : k + 1, :] = east[r : r + 1, :]
    for o in range(2):
        nw[8 * o : 8 * o + 8, :] = jnp.take_along_axis(nw[8 * o : 8 * o + 8, :], swap, axis=1)
        ne[8 * o : 8 * o + 8, :] = jnp.take_along_axis(ne[8 * o : 8 * o + 8, :], swap, axis=1)


def pack(links, field, kx, ky, sea):
    f32 = jnp.float32
    shapes = [(SIDE, 128), (SIDE, 128), (PLANES, 16, SIDE), (16, 128), (16, 128)]
    return pl.pallas_call(
        pack_kernel,
        out_shape=[jax.ShapeDtypeStruct(s, f32) for s in shapes],
        grid=(SIDE // PACK_ROWS,),
        in_specs=[SMEM]
        + [pl.BlockSpec((LEV, PACK_ROWS, SIDE), lambda i: (0, i, 0))]
        + [pl.BlockSpec((PACK_ROWS, SIDE), lambda i: (i, 0))] * 3,
        out_specs=[VMEM] * 5,
        scratch_shapes=[pltpu.VMEM((PLANES, 16, SIDE), f32)],
        compiler_params=pltpu.CompilerParams(vmem_limit_bytes=60 << 20),
        name="pack",
    )(links, field, kx, ky, sea)


EVEN, ODD = slice(0, 128), slice(128, 256)
HALVES = (EVEN, ODD)


def sorter():
    col = lax.broadcasted_iota(jnp.int32, (SIDE, SIDE), 0)
    at = lax.broadcasted_iota(jnp.int32, (SIDE, SIDE), 1)
    want = jnp.where(at < 128, 2 * at, 2 * at - 255)
    return (col == want).astype(jnp.float32).astype(jnp.bfloat16)


def sort_columns(x, right):
    big = x.astype(jnp.bfloat16)
    small = (x - big.astype(jnp.float32)).astype(jnp.bfloat16)
    return jnp.dot(big, right, preferred_element_type=jnp.float32) + jnp.dot(
        small, right, preferred_element_type=jnp.float32
    )


def wide_weights(sea, kx, ky, rows, we, ww, wn):
    lane, sub = lanes(), sublanes()
    for t in range(rows):
        s = [sea(t, h) for h in range(2)]
        x = [kx(t, h) for h in range(2)]
        we[t, :, EVEN] = 0.5 * (x[0] + x[1]) * s[0] * s[1]
        w = 0.5 * (x[1] + roll(x[0], -1)) * s[1] * roll(s[0], -1)
        w = jnp.where(lane == 127, 0.0, w)
        we[t, :, ODD] = w
        ww[t] = roll(w, 1)
        for h in range(2):
            if t < rows - 1:
                sn, yn = sea(t + 1, h), ky(t + 1, h)
            else:
                sn, yn = up(sea(0, h)), up(ky(0, h))
            w = 0.5 * (ky(t, h) + yn) * s[h] * sn
            if t == rows - 1:
                w = jnp.where(sub == 7, 0.0, w)
            wn[t, :, HALVES[h]] = w


def wide_step(src, dst, we, ww, wn, rows, levels):
    below = []
    for l in levels:
        for h in HALVES:
            over = up(src[l, 0, :, h])
            src[l, rows, :, h] = over
            below.append(down(wn[rows - 1, :, h] * (over - src[l, rows - 1, :, h])))
    here = [src[l, 0, :, h] for l in levels for h in HALVES]
    for t in range(rows):
        e = [we[t, :, h] for h in HALVES]
        n = [wn[t, :, h] for h in HALVES]
        w = ww[t]
        nxt = [src[l, t + 1, :, h] for l in levels for h in HALVES]
        flux = [n[i % 2] * (nxt[i] - here[i]) for i in range(len(here))]
        for i, l in zip(range(0, len(here), 2), levels):
            a, b = here[i : i + 2]
            f = e[0] * (b - a)
            dst[l, t, :, EVEN] = (a + f) + w * (roll(b, 1) - a) + (flux[i] - below[i])
            dst[l, t, :, ODD] = (b - f) + e[1] * (roll(a, -1) - b) + (flux[i + 1] - below[i + 1])
        here, below = nxt, flux


def mixing(vertical):
    levels = vertical.shape[0]
    size = 16 * levels

    def at(shape, axis):
        return lax.broadcasted_iota(jnp.int32, shape, axis)

    left = (at((size, levels), 0) // 16 == at((size, levels), 1)).astype(jnp.float32).astype(jnp.bfloat16)
    right = (at((levels, size), 1) // 16 == at((levels, size), 0)).astype(jnp.float32).astype(jnp.bfloat16)
    tall = jnp.dot(left, vertical, preferred_element_type=jnp.float32).astype(jnp.bfloat16)
    full = jnp.dot(tall, right, preferred_element_type=jnp.float32)
    same = at((size, size), 0) % 16 == at((size, size), 1) % 16
    return jnp.where(same, full, 0.0).astype(jnp.bfloat16)


def own_tile(low, high, i):
    group = lanes() // 32
    a, b = TILES[i]
    x = jnp.where(group == 0, roll(low[a], HALO), roll(high[a], 32 - 108))
    y = jnp.where(group == 2, roll(low[b], 64 + HALO), roll(high[b], 96 - 108))
    return jnp.where(group < 2, x, y)


def inner_kernel(*refs):
    field, kx, ky, sea = paired(refs[:8])
    vertical, cur, own, top, mixer, other, raw, st, we, ww, wn = refs[8:]
    for t in range(ROWS):
        low = planes_at(field, kx, ky, sea, t, 0)
        high = planes_at(field, kx, ky, sea, t, 1)
        for p in range(PLANES):
            raw[p, t, :, 0:128] = low[p]
            raw[p, t, :, 128:256] = high[p]
        for i in range(4):
            own[i, t] = own_tile(low, high, i)
    right = sorter()
    for p in range(PLANES):
        x = sort_columns(raw[p].reshape(SIDE, SIDE), right).reshape(ROWS, 8, SIDE)
        if p < LEV:
            cur[p, 0:ROWS] = x
        else:
            st[p - LEV] = x

    def plane(p):
        return lambda t, h: st[p, t, :, HALVES[h]]

    wide_weights(plane(0), plane(1), plane(2), ROWS, we, ww, wn)
    for h in range(2):
        cols = slice(128 * h, 128 * h + 128)
        land = sea[h][SIDE - TOP :, :].astype(jnp.float32)
        for l in range(LEV):
            top[l, :, cols] = field[h][l, SIDE - TOP :, :] * land
        top[LEV, :, cols] = land
        top[LEV + 1, :, cols] = kx[h][SIDE - TOP :, :]
        top[LEV + 2, :, cols] = ky[h][SIDE - TOP :, :]
    mixer[...] = mixing(vertical[...])

    def two_steps(_, none):
        wide_step(cur, other, we, ww, wn, ROWS, range(LEV))
        wide_step(other, cur, we, ww, wn, ROWS, range(LEV))
        return none

    lax.fori_loop(0, STEPS // 2, two_steps, 0)


def inner(field, kx, ky, sea, vertical):
    f32 = jnp.float32
    scratch = [
        (LEV, ROWS + 1, 8, SIDE),
        (PLANES, ROWS, 8, SIDE),
        (3, ROWS, 8, SIDE),
        (ROWS, 8, SIDE),
        (ROWS, 8, 128),
        (ROWS, 8, SIDE),
    ]
    shapes = [(LEV, ROWS + 1, 8, SIDE), (4, ROWS, 8, 128), (PLANES, TOP, SIDE)]
    return pl.pallas_call(
        inner_kernel,
        out_shape=[jax.ShapeDtypeStruct(s, f32) for s in shapes] + [jax.ShapeDtypeStruct((640, 640), jnp.bfloat16)],
        grid=(1,),
        in_specs=half_specs((LEV,), (), (), ()) + [VMEM],
        out_specs=[VMEM] * 4,
        scratch_shapes=[pltpu.VMEM(s, f32) for s in scratch],
        compiler_params=pltpu.CompilerParams(vmem_limit_bytes=24 << 20),
        cost_estimate=pl.CostEstimate(flops=40_000_000, bytes_accessed=40_000_000, transcendentals=0),
        name="inner",
    )(*doubled(field, kx, ky, sea), vertical)


def strip_step(src, dst, we, ww, wn, tiles):
    sub = sublanes()
    below = []
    for k in tiles:
        over = jnp.where(sub == 7, src[k, ROWS], up(src[k, 0]))
        src[k, ROWS] = over
        below.append(jnp.where(sub == 0, 0.0, down(wn[ROWS - 1] * (over - src[k, ROWS - 1]))))
    here = [src[k, 0] for k in tiles]
    for t in range(STRIP):
        e, w, n = we[t], ww[t], wn[t]
        nxt = [src[k, t + 1] for k in tiles]
        flux = [n * (x - c) for x, c in zip(nxt, here)]
        for k, c, f, g in zip(tiles, here, flux, below):
            dst[k, t] = c + e * (roll(c, -1) - c) + w * (roll(c, 1) - c) + (f - g)
        here, below = nxt, flux


def rim_kernel(links, inside, own, top, west, east, north, nw, ne, out, cur, other, we, ww, wn, kap, sea, ext, nbr, nb_even, nb_odd, nc, n_other, nwe, nww, nwn):
    lane, sub = lanes(), sublanes()
    group, part = lane // 32, lane % 32
    w_halo = (part < HALO) & (group % 2 == 0)
    e_halo = (part >= 20) & (group % 2 == 1)
    ones = jnp.ones((8, 128), jnp.float32)

    def with_halo(i, mine, w, e):
        x = jnp.where(w_halo, roll(w, W_SHIFT[i]), mine)
        return jnp.where(e_halo, roll(e, E_SHIFT[i]), x)

    strips = (cur.at[0], cur.at[1], cur.at[2], kap)
    def fill(b, none):
        for j in range(8):
            t = 8 * b + j
            at = pl.ds(t, 8, stride=ROWS)
            w, e = west[at, :], east[at, :]
            for i in range(4):
                strips[i][t] = with_halo(i, own[i, t], w, e)
        return none

    lax.fori_loop(0, ROWS // 8, fill, 0)
    for o in range(2):
        rows = slice(8 * o, 8 * o + 8)
        low = [north[p, rows, 0:128] for p in range(PLANES)]
        high = [north[p, rows, 128:256] for p in range(PLANES)]
        for i in range(4):
            ext[i, rows, :] = with_halo(i, own_tile(low, high, i), nw[rows, :], ne[rows, :])
    for k in range(DEPTH):
        for i in range(4):
            strips[i][ROWS + k] = jnp.broadcast_to(ext[i, k : k + 1, :], (8, 128))

    def flag(x):
        return jnp.where(x >= 0, 1.0, 0.0).astype(jnp.float32)

    w_open = ones * flag(links[0, 0])
    e_open = ones * flag(links[0, 1])
    w_over = jnp.broadcast_to(north[LEV, 15:16, 0:128], (8, 128))
    e_over = jnp.broadcast_to(north[LEV, 14:15, 0:128], (8, 128))
    seams = []
    for a, b in ((w_open, e_open), (w_over, e_over)):
        m = jnp.where(lane == HALO - 1, a, jnp.where(lane == 32 + 19, b, 1.0))
        seams.append(0.5 * jnp.where(part == 31, 0.0, m))
    first = group < 2
    def spread_sea(b, none):
        for j in range(14):
            c = cur[2, 14 * b + j]
            sea[14 * b + j] = jnp.where(first, roll(c, 64), c)
        return none

    lax.fori_loop(0, STRIP // 14, spread_sea, 0)

    def weights(t, seam, s, x, sn, yn):
        w = seam * (x + roll(x, -1)) * s * roll(s, -1)
        w = jnp.where(first, w, roll(w, 64))
        we[t] = w
        ww[t] = roll(w, 1)
        w = 0.5 * (x + yn) * s * sn
        wn[t] = jnp.where(first, roll(w, 64), w)

    def most_weights(b, none):
        for j in range(14):
            t = 14 * b + j
            weights(t, seams[0], sea[t], kap[t], sea[t + 1], kap[t + 1])
        return none

    lax.fori_loop(0, 2, most_weights, 0)
    for t in range(28, STRIP):
        s, x = sea[t], kap[t]
        sn, yn = (sea[t + 1], kap[t + 1]) if t < STRIP - 1 else (s, x)
        if t == ROWS - 1:
            sn = jnp.where(sub == 7, sn, up(sea[0]))
            yn = jnp.where(sub == 7, yn, up(kap[0]))
        weights(t, seams[t >= ROWS], s, x, sn, yn)
    zeros = jnp.zeros((8, 128), jnp.float32)
    wn[STRIP - 1] = zeros
    for i in range(3):
        cur[i, STRIP] = zeros
        other[i, STRIP] = zeros

    nbr[:, 0:TOP, :] = top[...]
    nbr[:, TOP : TOP + 16, :] = north[...]
    x = sort_columns(nbr[...].reshape(PLANES * (TOP + 16), SIDE), sorter()).reshape(PLANES, TOP + 16, SIDE)
    nb = (nb_even, nb_odd)
    for h in range(2):
        nb[h][...] = x[:, :, HALVES[h]]
    for l in range(LEV):
        for t in range(NORTH):
            for h in range(2):
                nc[l, t, :, HALVES[h]] = strided(nb, (l,), t, h, NORTH)

    def plane(p):
        return lambda t, h: strided(nb, (p,), t, h, NORTH)

    wide_weights(plane(LEV), plane(LEV + 1), plane(LEV + 2), NORTH, nwe, nww, nwn)

    def two_steps(_, none):
        strip_step(cur, other, we, ww, wn, range(3))
        wide_step(nc, n_other, nwe, nww, nwn, NORTH, range(LEV))
        strip_step(other, cur, we, ww, wn, range(3))
        wide_step(n_other, nc, nwe, nww, nwn, NORTH, range(LEV))
        return none

    lax.fori_loop(0, STEPS // 2, two_steps, 0)

    for l in range(LEV):
        for t in range(NORTH):
            for h in range(2):
                nb[h][l, pl.ds(t, 8, stride=NORTH), :] = nc[l, t, :, HALVES[h]]

    on_rim = (lane < 5) | (lane >= 123)
    top_row = sub == 7
    for l in range(LEV):
        i, base = l // 2, 64 * (l % 2)
        pick = [
            jnp.where(lane < 5, base + HALO + 2 * lane + h, jnp.where(lane >= 123, base + 42 + 2 * (lane - 123) + h, 0))
            for h in range(2)
        ]
        for t in range(0, ROWS, 2):
            pair = []
            for u in (t, t + 1):
                for h in range(2):
                    x = inside[l, u, :, HALVES[h]]
                    if u >= ROWS - DEPTH:
                        r = TOP - ROWS + u
                        x = jnp.where(top_row, jnp.broadcast_to(nb[h][l, r : r + 1, :], (8, 128)), x)
                    pair.append(jnp.where(on_rim, jnp.take_along_axis(cur[i, u], pick[h], axis=1), x))
            q, r = t // 4, 8 * (t % 4)
            for h in range(2):
                x = jnp.concatenate([pair[h], pair[2 + h]], axis=0)
                out[q, l, r : r + 16, HALVES[h]] = x.astype(jnp.bfloat16)


def rim(links, inside, own, top, west, east, north, nw, ne):
    f32 = jnp.float32
    scratch = [
        (3, STRIP + 1, 8, 128),
        (3, STRIP + 1, 8, 128),
        (STRIP, 8, 128),
        (STRIP, 8, 128),
        (STRIP, 8, 128),
        (STRIP, 8, 128),
        (STRIP, 8, 128),
        (4, 16, 128),
        (PLANES, TOP + 16, SIDE),
        (PLANES, TOP + 16, 128),
        (PLANES, TOP + 16, 128),
        (LEV, NORTH + 1, 8, SIDE),
        (LEV, NORTH + 1, 8, SIDE),
        (NORTH, 8, SIDE),
        (NORTH, 8, 128),
        (NORTH, 8, SIDE),
    ]
    return pl.pallas_call(
        rim_kernel,
        out_shape=jax.ShapeDtypeStruct((CHUNKS, LEV, SIDE // CHUNKS, SIDE), jnp.bfloat16),
        in_specs=[SMEM] + [VMEM] * 8,
        out_specs=VMEM,
        scratch_shapes=[pltpu.VMEM(s, f32) for s in scratch],
        compiler_params=pltpu.CompilerParams(vmem_limit_bytes=24 << 20),
        name="rim",
    )(links, inside, own, top, west, east, north, nw, ne)


def mix_kernel(x, k, y):
    for h in range(2):
        rows = x[:, :, 16 * h : 16 * h + 16, :].reshape(CHUNKS * LEV * 16, SIDE)
        mixed = jnp.dot(k[...], rows, preferred_element_type=jnp.float32).astype(jnp.bfloat16)
        y[:, :, 16 * h : 16 * h + 16, :] = mixed.reshape(CHUNKS, LEV, 16, SIDE)


def mix(x, k):
    return pl.pallas_call(
        mix_kernel,
        out_shape=jax.ShapeDtypeStruct(x.shape, jnp.bfloat16),
        in_specs=[VMEM] * 2,
        out_specs=VMEM,
        compiler_params=pltpu.CompilerParams(vmem_limit_bytes=24 << 20),
        name="mix",
    )(x, k)


def unpack_kernel(z, out):
    at = lax.broadcasted_iota(jnp.int32, (SIDE, 128), 0)
    col = lax.broadcasted_iota(jnp.int32, (SIDE, 128), 1) + 128 * pl.program_id(0)
    back = (jnp.where(at < 128, 2 * at, 2 * at - 255) == col).astype(jnp.float32).astype(jnp.bfloat16)
    for q in range(CHUNKS):
        x = jnp.dot(z[q].reshape(LEV * 32, SIDE), back, preferred_element_type=jnp.float32)
        for l in range(LEV):
            for u in range(4):
                r = 32 * l + 8 * u
                out[l, pl.ds(4 * q + u, 8, stride=ROWS), :] = x[r : r + 8]


def unpack(z):
    return pl.pallas_call(
        unpack_kernel,
        out_shape=jax.ShapeDtypeStruct((LEV, SIDE, SIDE), jnp.float32),
        grid=(2,),
        in_specs=[pl.BlockSpec((CHUNKS, LEV, SIDE // CHUNKS, SIDE), lambda h: (0, 0, 0, 0))],
        out_specs=pl.BlockSpec((LEV, SIDE, 128), lambda h: (0, 0, h)),
        compiler_params=pltpu.CompilerParams(vmem_limit_bytes=24 << 20),
        name="unpack",
    )(z)


def shards(field, kappa_x, kappa_y, sea_mask, tile_links, vertical):
    tiles = lax.axis_size("tile")

    def send(x, target):
        return lax.ppermute(x, "tile", [(i, target(i) % tiles) for i in range(tiles)])

    cells, kx, ky, sea = field[0], kappa_x[0], kappa_y[0], sea_mask[0]
    west, east, north, nw, ne = pack(tile_links, cells, kx, ky, sea)
    from_east = send(west, lambda i: i - 1)
    from_west = send(east, lambda i: i + 1)
    from_north = send(north, lambda i: -i)
    from_nw = send(nw, lambda i: 1 - i)
    from_ne = send(ne, lambda i: -1 - i)
    inside, own, top, mixer = inner(cells, kx, ky, sea, vertical)
    smooth = rim(tile_links, inside, own, top, from_west, from_east, from_north, from_nw, from_ne)
    gathered = lax.all_to_all(smooth, "lev", 0, 0, tiled=True)
    back = lax.all_to_all(mix(gathered, mixer), "lev", 0, 0, tiled=True)
    return unpack(back)[None]


def solution(mesh):
    placed = (
        P("tile", "lev", None, None),
        P("tile", None, None),
        P("tile", None, None),
        P("tile", None, None),
        P("tile", None),
        P(),
    )
    return jax.shard_map(
        shards, mesh=mesh, in_specs=placed, out_specs=P("tile", "lev", None, None), check_vma=False
    )
```

```python
import jax
import jax.numpy as jnp
from jax import lax
from jax.experimental import pallas as pl
from jax.experimental.pallas import tpu as pltpu
from jax.sharding import PartitionSpec as P

STEPS = 10
LEV = 5
PLANES = LEV + 3
SIDE = 256
ROWS = 32
HALO = 12
DEPTH = 10
STRIP = ROWS + DEPTH
TOP = 24
NORTH = 5
CHUNKS = 8
PACK_ROWS = 128
SLOT = (0, 4, 2, 6, 1, 5, 3, 7)
TILES = ((0, 1), (2, 3), (4, 5), (6, 7))
W_SHIFT = (-4, -36, -20, -52)
E_SHIFT = (52, 20, 36, 4)

VMEM = pl.BlockSpec(memory_space=pltpu.VMEM)
SMEM = pl.BlockSpec(memory_space=pltpu.SMEM)


def lanes():
    return lax.broadcasted_iota(jnp.int32, (8, 128), 1)


def sublanes():
    return lax.broadcasted_iota(jnp.int32, (8, 128), 0)


def roll(x, shift):
    shift = shift % 128
    return x if shift == 0 else pltpu.roll(x, shift, 1)


def up(x):
    return pltpu.roll(x, 7, 0)


def down(x):
    return pltpu.roll(x, 1, 0)


def strided(halves, lead, t, half, stride):
    return halves[half][(*lead, pl.ds(t, 8, stride=stride), slice(None))]


def half_specs(*leads):
    return [
        pl.BlockSpec((*lead, SIDE, 128), lambda i, n=len(lead), h=h: (0,) * (n + 1) + (h,))
        for lead in leads
        for h in range(2)
    ]


def doubled(*arrays):
    return [a for a in arrays for _ in range(2)]


def paired(refs):
    return [refs[i : i + 2] for i in range(0, len(refs), 2)]


def planes_at(field, kx, ky, sea, t, half):
    land = strided(sea, (), t, half, ROWS).astype(jnp.float32)
    out = [strided(field, (l,), t, half, ROWS) * land for l in range(LEV)]
    return out + [land, strided(kx, (), t, half, ROWS), strided(ky, (), t, half, ROWS)]


def pack_kernel(links, field, kx, ky, sea, west, east, north, nw, ne, rows):
    lane = lanes()
    group = lane // 16
    start = PACK_ROWS * pl.program_id(0)

    def planes(at, cols):
        land = sea[at, cols].astype(jnp.float32)
        return [field[l, at, cols] * land for l in range(LEV)] + [land, kx[at, cols], ky[at, cols]]

    for t in range(PACK_ROWS // 8):
        at = slice(8 * t, 8 * t + 8)
        low, high = planes(at, slice(0, 128)), planes(at, slice(128, 256))
        w, e = low[0], roll(high[0], 16)
        for p in range(1, PLANES):
            w = jnp.where(group == SLOT[p], roll(low[p], 16 * SLOT[p]), w)
            e = jnp.where(group == SLOT[p], roll(high[p], 16 * SLOT[p] + 16), e)
        to = pl.ds(pl.multiple_of(start + 8 * t, 8), 8)
        west[to, :] = w
        east[to, :] = e

    @pl.when(pl.program_id(0) == SIDE // PACK_ROWS - 1)
    def _():
        pack_top(links, planes, west, east, north, nw, ne, rows)


def pack_top(links, planes, west, east, north, nw, ne, rows):
    lane = lanes()
    flip = 127 - lane
    for o in range(2):
        for half in range(2):
            at = slice(PACK_ROWS - 16 + 8 * o, PACK_ROWS - 8 + 8 * o)
            for p, x in enumerate(planes(at, slice(128 * half, 128 * half + 128))):
                x = jnp.take_along_axis(x, flip, axis=1)
                rows[p, 8 * o : 8 * o + 8, 128 * (1 - half) : 128 * (1 - half) + 128] = x
    for k in range(16):
        north[:, k, :] = rows[:, 15 - k, :]
    west_open = jnp.where(links[0, 0] >= 0, 1.0, 0.0).astype(jnp.float32)
    east_open = jnp.where(links[0, 1] >= 0, 1.0, 0.0).astype(jnp.float32)
    north[LEV, 14, :] = jnp.full((SIDE,), 1.0, jnp.float32) * west_open
    north[LEV, 15, :] = jnp.full((SIDE,), 1.0, jnp.float32) * east_open
    swap = jnp.bitwise_xor(lane, 15)
    for k in range(16):
        r = SIDE - 1 - k
        nw[k : k + 1, :] = west[r : r + 1, :]
        ne[k : k + 1, :] = east[r : r + 1, :]
    for o in range(2):
        nw[8 * o : 8 * o + 8, :] = jnp.take_along_axis(nw[8 * o : 8 * o + 8, :], swap, axis=1)
        ne[8 * o : 8 * o + 8, :] = jnp.take_along_axis(ne[8 * o : 8 * o + 8, :], swap, axis=1)


def pack(links, field, kx, ky, sea):
    f32 = jnp.float32
    shapes = [(SIDE, 128), (SIDE, 128), (PLANES, 16, SIDE), (16, 128), (16, 128)]
    return pl.pallas_call(
        pack_kernel,
        out_shape=[jax.ShapeDtypeStruct(s, f32) for s in shapes],
        grid=(SIDE // PACK_ROWS,),
        in_specs=[SMEM]
        + [pl.BlockSpec((LEV, PACK_ROWS, SIDE), lambda i: (0, i, 0))]
        + [pl.BlockSpec((PACK_ROWS, SIDE), lambda i: (i, 0))] * 3,
        out_specs=[VMEM] * 5,
        scratch_shapes=[pltpu.VMEM((PLANES, 16, SIDE), f32)],
        compiler_params=pltpu.CompilerParams(vmem_limit_bytes=60 << 20),
        name="pack",
    )(links, field, kx, ky, sea)


EVEN, ODD = slice(0, 128), slice(128, 256)
HALVES = (EVEN, ODD)


def sorter():
    col = lax.broadcasted_iota(jnp.int32, (SIDE, SIDE), 0)
    at = lax.broadcasted_iota(jnp.int32, (SIDE, SIDE), 1)
    want = jnp.where(at < 128, 2 * at, 2 * at - 255)
    return (col == want).astype(jnp.float32).astype(jnp.bfloat16)


def sort_columns(x, right):
    big = x.astype(jnp.bfloat16)
    small = (x - big.astype(jnp.float32)).astype(jnp.bfloat16)
    return jnp.dot(big, right, preferred_element_type=jnp.float32) + jnp.dot(
        small, right, preferred_element_type=jnp.float32
    )


def wide_weights(sea, kx, ky, rows, we, ww, wn):
    lane, sub = lanes(), sublanes()
    for t in range(rows):
        s = [sea(t, h) for h in range(2)]
        x = [kx(t, h) for h in range(2)]
        we[t, :, EVEN] = 0.5 * (x[0] + x[1]) * s[0] * s[1]
        w = 0.5 * (x[1] + roll(x[0], -1)) * s[1] * roll(s[0], -1)
        w = jnp.where(lane == 127, 0.0, w)
        we[t, :, ODD] = w
        ww[t] = roll(w, 1)
        for h in range(2):
            if t < rows - 1:
                sn, yn = sea(t + 1, h), ky(t + 1, h)
            else:
                sn, yn = up(sea(0, h)), up(ky(0, h))
            w = 0.5 * (ky(t, h) + yn) * s[h] * sn
            if t == rows - 1:
                w = jnp.where(sub == 7, 0.0, w)
            wn[t, :, HALVES[h]] = w


def wide_step(src, dst, we, ww, wn, rows, levels):
    below = []
    for l in levels:
        for h in HALVES:
            over = up(src[l, 0, :, h])
            src[l, rows, :, h] = over
            below.append(down(wn[rows - 1, :, h] * (over - src[l, rows - 1, :, h])))
    here = [src[l, 0, :, h] for l in levels for h in HALVES]
    for t in range(rows):
        e = [we[t, :, h] for h in HALVES]
        n = [wn[t, :, h] for h in HALVES]
        w = ww[t]
        nxt = [src[l, t + 1, :, h] for l in levels for h in HALVES]
        flux = [n[i % 2] * (nxt[i] - here[i]) for i in range(len(here))]
        for i, l in zip(range(0, len(here), 2), levels):
            a, b = here[i : i + 2]
            f = e[0] * (b - a)
            dst[l, t, :, EVEN] = (a + f) + w * (roll(b, 1) - a) + (flux[i] - below[i])
            dst[l, t, :, ODD] = (b - f) + e[1] * (roll(a, -1) - b) + (flux[i + 1] - below[i + 1])
        here, below = nxt, flux


def mixing(vertical):
    levels = vertical.shape[0]
    size = 16 * levels

    def at(shape, axis):
        return lax.broadcasted_iota(jnp.int32, shape, axis)


    def level(row):
        return LEV * (CHUNKS - 1 - row // (16 * LEV)) + row // 16 % LEV

    left = (level(at((size, levels), 0)) == at((size, levels), 1)).astype(jnp.float32).astype(jnp.bfloat16)
    right = (level(at((levels, size), 1)) == at((levels, size), 0)).astype(jnp.float32).astype(jnp.bfloat16)
    tall = jnp.dot(left, vertical, preferred_element_type=jnp.float32).astype(jnp.bfloat16)
    full = jnp.dot(tall, right, preferred_element_type=jnp.float32)
    same = at((size, size), 0) % 16 == at((size, size), 1) % 16
    return jnp.where(same, full, 0.0).astype(jnp.bfloat16)


def own_tile(low, high, i):
    group = lanes() // 32
    a, b = TILES[i]
    x = jnp.where(group == 0, roll(low[a], HALO), roll(high[a], 32 - 108))
    y = jnp.where(group == 2, roll(low[b], 64 + HALO), roll(high[b], 96 - 108))
    return jnp.where(group < 2, x, y)


def inner_kernel(*refs):
    field, kx, ky, sea = paired(refs[:8])
    vertical, cur, own, top, mixer, other, raw, st, we, ww, wn = refs[8:]
    for t in range(ROWS):
        low = planes_at(field, kx, ky, sea, t, 0)
        high = planes_at(field, kx, ky, sea, t, 1)
        for p in range(PLANES):
            raw[p, t, :, 0:128] = low[p]
            raw[p, t, :, 128:256] = high[p]
        for i in range(4):
            own[i, t] = own_tile(low, high, i)
    right = sorter()
    for p in range(PLANES):
        x = sort_columns(raw[p].reshape(SIDE, SIDE), right).reshape(ROWS, 8, SIDE)
        if p < LEV:
            cur[p, 0:ROWS] = x
        else:
            st[p - LEV] = x

    def plane(p):
        return lambda t, h: st[p, t, :, HALVES[h]]

    wide_weights(plane(0), plane(1), plane(2), ROWS, we, ww, wn)
    for h in range(2):
        cols = slice(128 * h, 128 * h + 128)
        land = sea[h][SIDE - TOP :, :].astype(jnp.float32)
        for l in range(LEV):
            top[l, :, cols] = field[h][l, SIDE - TOP :, :] * land
        top[LEV, :, cols] = land
        top[LEV + 1, :, cols] = kx[h][SIDE - TOP :, :]
        top[LEV + 2, :, cols] = ky[h][SIDE - TOP :, :]
    mixer[...] = mixing(vertical[...])

    def two_steps(_, none):
        wide_step(cur, other, we, ww, wn, ROWS, range(LEV))
        wide_step(other, cur, we, ww, wn, ROWS, range(LEV))
        return none

    lax.fori_loop(0, STEPS // 2, two_steps, 0)


def inner(field, kx, ky, sea, vertical):
    f32 = jnp.float32
    scratch = [
        (LEV, ROWS + 1, 8, SIDE),
        (PLANES, ROWS, 8, SIDE),
        (3, ROWS, 8, SIDE),
        (ROWS, 8, SIDE),
        (ROWS, 8, 128),
        (ROWS, 8, SIDE),
    ]
    shapes = [(LEV, ROWS + 1, 8, SIDE), (4, ROWS, 8, 128), (PLANES, TOP, SIDE)]
    return pl.pallas_call(
        inner_kernel,
        out_shape=[jax.ShapeDtypeStruct(s, f32) for s in shapes] + [jax.ShapeDtypeStruct((640, 640), jnp.bfloat16)],
        grid=(1,),
        in_specs=half_specs((LEV,), (), (), ()) + [VMEM],
        out_specs=[VMEM] * 4,
        scratch_shapes=[pltpu.VMEM(s, f32) for s in scratch],
        compiler_params=pltpu.CompilerParams(vmem_limit_bytes=24 << 20),
        cost_estimate=pl.CostEstimate(flops=40_000_000, bytes_accessed=40_000_000, transcendentals=0),
        name="inner",
    )(*doubled(field, kx, ky, sea), vertical)


def strip_step(src, dst, we, ww, wn, tiles):
    sub = sublanes()
    below = []
    for k in tiles:
        over = jnp.where(sub == 7, src[k, ROWS], up(src[k, 0]))
        src[k, ROWS] = over
        below.append(jnp.where(sub == 0, 0.0, down(wn[ROWS - 1] * (over - src[k, ROWS - 1]))))
    here = [src[k, 0] for k in tiles]
    for t in range(STRIP):
        e, w, n = we[t], ww[t], wn[t]
        nxt = [src[k, t + 1] for k in tiles]
        flux = [n * (x - c) for x, c in zip(nxt, here)]
        for k, c, f, g in zip(tiles, here, flux, below):
            dst[k, t] = c + e * (roll(c, -1) - c) + w * (roll(c, 1) - c) + (f - g)
        here, below = nxt, flux


def rim_kernel(links, inside, own, top, west, east, north, nw, ne, out, cur, other, we, ww, wn, kap, sea, ext, nbr, nb_even, nb_odd, nc, n_other, nwe, nww, nwn):
    lane, sub = lanes(), sublanes()
    group, part = lane // 32, lane % 32
    w_halo = (part < HALO) & (group % 2 == 0)
    e_halo = (part >= 20) & (group % 2 == 1)
    ones = jnp.ones((8, 128), jnp.float32)

    def with_halo(i, mine, w, e):
        x = jnp.where(w_halo, roll(w, W_SHIFT[i]), mine)
        return jnp.where(e_halo, roll(e, E_SHIFT[i]), x)

    strips = (cur.at[0], cur.at[1], cur.at[2], kap)
    def fill(b, none):
        for j in range(8):
            t = 8 * b + j
            at = pl.ds(t, 8, stride=ROWS)
            w, e = west[at, :], east[at, :]
            for i in range(4):
                strips[i][t] = with_halo(i, own[i, t], w, e)
        return none

    lax.fori_loop(0, ROWS // 8, fill, 0)
    for o in range(2):
        rows = slice(8 * o, 8 * o + 8)
        low = [north[p, rows, 0:128] for p in range(PLANES)]
        high = [north[p, rows, 128:256] for p in range(PLANES)]
        for i in range(4):
            ext[i, rows, :] = with_halo(i, own_tile(low, high, i), nw[rows, :], ne[rows, :])
    for k in range(DEPTH):
        for i in range(4):
            strips[i][ROWS + k] = jnp.broadcast_to(ext[i, k : k + 1, :], (8, 128))

    def flag(x):
        return jnp.where(x >= 0, 1.0, 0.0).astype(jnp.float32)

    w_open = ones * flag(links[0, 0])
    e_open = ones * flag(links[0, 1])
    w_over = jnp.broadcast_to(north[LEV, 15:16, 0:128], (8, 128))
    e_over = jnp.broadcast_to(north[LEV, 14:15, 0:128], (8, 128))
    seams = []
    for a, b in ((w_open, e_open), (w_over, e_over)):
        m = jnp.where(lane == HALO - 1, a, jnp.where(lane == 32 + 19, b, 1.0))
        seams.append(0.5 * jnp.where(part == 31, 0.0, m))
    first = group < 2
    def spread_sea(b, none):
        for j in range(14):
            c = cur[2, 14 * b + j]
            sea[14 * b + j] = jnp.where(first, roll(c, 64), c)
        return none

    lax.fori_loop(0, STRIP // 14, spread_sea, 0)

    def weights(t, seam, s, x, sn, yn):
        w = seam * (x + roll(x, -1)) * s * roll(s, -1)
        w = jnp.where(first, w, roll(w, 64))
        we[t] = w
        ww[t] = roll(w, 1)
        w = 0.5 * (x + yn) * s * sn
        wn[t] = jnp.where(first, roll(w, 64), w)

    def most_weights(b, none):
        for j in range(14):
            t = 14 * b + j
            weights(t, seams[0], sea[t], kap[t], sea[t + 1], kap[t + 1])
        return none

    lax.fori_loop(0, 2, most_weights, 0)
    for t in range(28, STRIP):
        s, x = sea[t], kap[t]
        sn, yn = (sea[t + 1], kap[t + 1]) if t < STRIP - 1 else (s, x)
        if t == ROWS - 1:
            sn = jnp.where(sub == 7, sn, up(sea[0]))
            yn = jnp.where(sub == 7, yn, up(kap[0]))
        weights(t, seams[t >= ROWS], s, x, sn, yn)
    zeros = jnp.zeros((8, 128), jnp.float32)
    wn[STRIP - 1] = zeros
    for i in range(3):
        cur[i, STRIP] = zeros
        other[i, STRIP] = zeros

    nbr[:, 0:TOP, :] = top[...]
    nbr[:, TOP : TOP + 16, :] = north[...]
    x = sort_columns(nbr[...].reshape(PLANES * (TOP + 16), SIDE), sorter()).reshape(PLANES, TOP + 16, SIDE)
    nb = (nb_even, nb_odd)
    for h in range(2):
        nb[h][...] = x[:, :, HALVES[h]]
    for l in range(LEV):
        for t in range(NORTH):
            for h in range(2):
                nc[l, t, :, HALVES[h]] = strided(nb, (l,), t, h, NORTH)

    def plane(p):
        return lambda t, h: strided(nb, (p,), t, h, NORTH)

    wide_weights(plane(LEV), plane(LEV + 1), plane(LEV + 2), NORTH, nwe, nww, nwn)

    def two_steps(_, none):
        strip_step(cur, other, we, ww, wn, range(3))
        wide_step(nc, n_other, nwe, nww, nwn, NORTH, range(LEV))
        strip_step(other, cur, we, ww, wn, range(3))
        wide_step(n_other, nc, nwe, nww, nwn, NORTH, range(LEV))
        return none

    lax.fori_loop(0, STEPS // 2, two_steps, 0)

    for l in range(LEV):
        for t in range(NORTH):
            for h in range(2):
                nb[h][l, pl.ds(t, 8, stride=NORTH), :] = nc[l, t, :, HALVES[h]]

    on_rim = (lane < 5) | (lane >= 123)
    top_row = sub == 7
    for l in range(LEV):
        i, base = l // 2, 64 * (l % 2)
        pick = [
            jnp.where(lane < 5, base + HALO + 2 * lane + h, jnp.where(lane >= 123, base + 42 + 2 * (lane - 123) + h, 0))
            for h in range(2)
        ]
        for t in range(0, ROWS, 2):
            pair = []
            for u in (t, t + 1):
                for h in range(2):
                    x = inside[l, u, :, HALVES[h]]
                    if u >= ROWS - DEPTH:
                        r = TOP - ROWS + u
                        x = jnp.where(top_row, jnp.broadcast_to(nb[h][l, r : r + 1, :], (8, 128)), x)
                    pair.append(jnp.where(on_rim, jnp.take_along_axis(cur[i, u], pick[h], axis=1), x))
            q, r = t // 4, 8 * (t % 4)
            for h in range(2):
                x = jnp.concatenate([pair[h], pair[2 + h]], axis=0)
                out[q, l, r : r + 16, HALVES[h]] = x.astype(jnp.bfloat16)


def rim(links, inside, own, top, west, east, north, nw, ne):
    f32 = jnp.float32
    scratch = [
        (3, STRIP + 1, 8, 128),
        (3, STRIP + 1, 8, 128),
        (STRIP, 8, 128),
        (STRIP, 8, 128),
        (STRIP, 8, 128),
        (STRIP, 8, 128),
        (STRIP, 8, 128),
        (4, 16, 128),
        (PLANES, TOP + 16, SIDE),
        (PLANES, TOP + 16, 128),
        (PLANES, TOP + 16, 128),
        (LEV, NORTH + 1, 8, SIDE),
        (LEV, NORTH + 1, 8, SIDE),
        (NORTH, 8, SIDE),
        (NORTH, 8, 128),
        (NORTH, 8, SIDE),
    ]
    return pl.pallas_call(
        rim_kernel,
        out_shape=jax.ShapeDtypeStruct((CHUNKS, LEV, SIDE // CHUNKS, SIDE), jnp.bfloat16),
        in_specs=[SMEM] + [VMEM] * 8,
        out_specs=VMEM,
        scratch_shapes=[pltpu.VMEM(s, f32) for s in scratch],
        compiler_params=pltpu.CompilerParams(vmem_limit_bytes=24 << 20),
        name="rim",
    )(links, inside, own, top, west, east, north, nw, ne)


def mix_kernel(x, k, y):
    for h in range(2):
        rows = x[:, :, 16 * h : 16 * h + 16, :].reshape(CHUNKS * LEV * 16, SIDE)
        mixed = jnp.dot(k[...], rows, preferred_element_type=jnp.float32).astype(jnp.bfloat16)
        y[:, :, 16 * h : 16 * h + 16, :] = mixed.reshape(CHUNKS, LEV, 16, SIDE)


def mix(x, k):
    return pl.pallas_call(
        mix_kernel,
        out_shape=jax.ShapeDtypeStruct(x.shape, jnp.bfloat16),
        in_specs=[VMEM] * 2,
        out_specs=VMEM,
        compiler_params=pltpu.CompilerParams(vmem_limit_bytes=24 << 20),
        name="mix",
    )(x, k)


def unpack_kernel(z, out):
    at = lax.broadcasted_iota(jnp.int32, (SIDE, 128), 0)
    col = lax.broadcasted_iota(jnp.int32, (SIDE, 128), 1) + 128 * pl.program_id(0)
    back = (jnp.where(at < 128, 2 * at, 2 * at - 255) == col).astype(jnp.float32).astype(jnp.bfloat16)
    for q in range(CHUNKS):
        x = jnp.dot(z[q].reshape(LEV * 32, SIDE), back, preferred_element_type=jnp.float32)
        for l in range(LEV):
            for u in range(4):
                r = 32 * l + 8 * u
                out[l, pl.ds(4 * q + u, 8, stride=ROWS), :] = x[r : r + 8]


def unpack(z):
    return pl.pallas_call(
        unpack_kernel,
        out_shape=jax.ShapeDtypeStruct((LEV, SIDE, SIDE), jnp.float32),
        grid=(2,),
        in_specs=[pl.BlockSpec((CHUNKS, LEV, SIDE // CHUNKS, SIDE), lambda h: (0, 0, 0, 0))],
        out_specs=pl.BlockSpec((LEV, SIDE, 128), lambda h: (0, 0, h)),
        compiler_params=pltpu.CompilerParams(vmem_limit_bytes=24 << 20),
        name="unpack",
    )(z)


def shards(field, kappa_x, kappa_y, sea_mask, tile_links, vertical):
    tiles = lax.axis_size("tile")

    def send(x, target):
        return lax.ppermute(x, "tile", [(i, target(i) % tiles) for i in range(tiles)])

    cells, kx, ky, sea = field[0], kappa_x[0], kappa_y[0], sea_mask[0]
    west, east, north, nw, ne = pack(tile_links, cells, kx, ky, sea)
    from_east = send(west, lambda i: i - 1)
    from_west = send(east, lambda i: i + 1)
    from_north = send(north, lambda i: -i)
    from_nw = send(nw, lambda i: 1 - i)
    from_ne = send(ne, lambda i: -1 - i)
    inside, own, top, mixer = inner(cells, kx, ky, sea, vertical)
    smooth = rim(tile_links, inside, own, top, from_west, from_east, from_north, from_nw, from_ne)

    def turn(x):
        return lax.all_to_all(x, "lev", 0, 0, axis_index_groups=[list(range(CHUNKS))[::-1]], tiled=True)

    return unpack(turn(mix(turn(smooth), mixer)))[None]


def solution(mesh):
    placed = (
        P("tile", "lev", None, None),
        P("tile", None, None),
        P("tile", None, None),
        P("tile", None, None),
        P("tile", None),
        P(),
    )
    return jax.shard_map(
        shards, mesh=mesh, in_specs=placed, out_specs=P("tile", "lev", None, None), check_vma=False
    )
```

```python
import jax
import jax.numpy as jnp
from jax import lax
from jax.experimental import pallas as pl
from jax.experimental.pallas import tpu as pltpu
from jax.sharding import PartitionSpec as P

STEPS = 10
LEV = 5
PLANES = LEV + 3
SIDE = 256
ROWS = 32
HALO = 12
DEPTH = 10
STRIP = ROWS + DEPTH
TOP = 24
NORTH = 5
CHUNKS = 8
PACK_ROWS = 128
SLOT = (0, 4, 2, 6, 1, 5, 3, 7)
TILES = ((0, 1), (2, 3), (4, 5), (6, 7))
W_SHIFT = (-4, -36, -20, -52)
E_SHIFT = (52, 20, 36, 4)

VMEM = pl.BlockSpec(memory_space=pltpu.VMEM)
SMEM = pl.BlockSpec(memory_space=pltpu.SMEM)


def lanes():
    return lax.broadcasted_iota(jnp.int32, (8, 128), 1)


def sublanes():
    return lax.broadcasted_iota(jnp.int32, (8, 128), 0)


def roll(x, shift):
    shift = shift % 128
    return x if shift == 0 else pltpu.roll(x, shift, 1)


def up(x):
    return pltpu.roll(x, 7, 0)


def down(x):
    return pltpu.roll(x, 1, 0)


def strided(halves, lead, t, half, stride):
    return halves[half][(*lead, pl.ds(t, 8, stride=stride), slice(None))]


def half_specs(*leads):
    return [
        pl.BlockSpec((*lead, SIDE, 128), lambda i, n=len(lead), h=h: (0,) * (n + 1) + (h,))
        for lead in leads
        for h in range(2)
    ]


def doubled(*arrays):
    return [a for a in arrays for _ in range(2)]


def paired(refs):
    return [refs[i : i + 2] for i in range(0, len(refs), 2)]


def planes_at(field, kx, ky, sea, t, half):
    land = strided(sea, (), t, half, ROWS).astype(jnp.float32)
    out = [strided(field, (l,), t, half, ROWS) * land for l in range(LEV)]
    return out + [land, strided(kx, (), t, half, ROWS), strided(ky, (), t, half, ROWS)]


def pack_kernel(links, field, kx, ky, sea, west, east, north, nw, ne, rows):
    lane = lanes()
    group = lane // 16
    start = PACK_ROWS * pl.program_id(0)

    def planes(at, cols):
        land = sea[at, cols].astype(jnp.float32)
        return [field[l, at, cols] * land for l in range(LEV)] + [land, kx[at, cols], ky[at, cols]]

    for t in range(PACK_ROWS // 8):
        at = slice(8 * t, 8 * t + 8)
        low, high = planes(at, slice(0, 128)), planes(at, slice(128, 256))
        w, e = low[0], roll(high[0], 16)
        for p in range(1, PLANES):
            w = jnp.where(group == SLOT[p], roll(low[p], 16 * SLOT[p]), w)
            e = jnp.where(group == SLOT[p], roll(high[p], 16 * SLOT[p] + 16), e)
        to = pl.ds(pl.multiple_of(start + 8 * t, 8), 8)
        west[to, :] = w
        east[to, :] = e

    @pl.when(pl.program_id(0) == SIDE // PACK_ROWS - 1)
    def _():
        pack_top(links, planes, west, east, north, nw, ne, rows)


def pack_top(links, planes, west, east, north, nw, ne, rows):
    lane = lanes()
    flip = 127 - lane
    for o in range(2):
        for half in range(2):
            at = slice(PACK_ROWS - 16 + 8 * o, PACK_ROWS - 8 + 8 * o)
            for p, x in enumerate(planes(at, slice(128 * half, 128 * half + 128))):
                x = jnp.take_along_axis(x, flip, axis=1)
                rows[p, 8 * o : 8 * o + 8, 128 * (1 - half) : 128 * (1 - half) + 128] = x
    for k in range(16):
        north[:, k, :] = rows[:, 15 - k, :]
    west_open = jnp.where(links[0, 0] >= 0, 1.0, 0.0).astype(jnp.float32)
    east_open = jnp.where(links[0, 1] >= 0, 1.0, 0.0).astype(jnp.float32)
    north[LEV, 14, :] = jnp.full((SIDE,), 1.0, jnp.float32) * west_open
    north[LEV, 15, :] = jnp.full((SIDE,), 1.0, jnp.float32) * east_open
    swap = jnp.bitwise_xor(lane, 15)
    for k in range(16):
        r = SIDE - 1 - k
        nw[k : k + 1, :] = west[r : r + 1, :]
        ne[k : k + 1, :] = east[r : r + 1, :]
    for o in range(2):
        nw[8 * o : 8 * o + 8, :] = jnp.take_along_axis(nw[8 * o : 8 * o + 8, :], swap, axis=1)
        ne[8 * o : 8 * o + 8, :] = jnp.take_along_axis(ne[8 * o : 8 * o + 8, :], swap, axis=1)


def pack(links, field, kx, ky, sea):
    f32 = jnp.float32
    shapes = [(SIDE, 128), (SIDE, 128), (PLANES, 16, SIDE), (16, 128), (16, 128)]
    return pl.pallas_call(
        pack_kernel,
        out_shape=[jax.ShapeDtypeStruct(s, f32) for s in shapes],
        grid=(SIDE // PACK_ROWS,),
        in_specs=[SMEM]
        + [pl.BlockSpec((LEV, PACK_ROWS, SIDE), lambda i: (0, i, 0))]
        + [pl.BlockSpec((PACK_ROWS, SIDE), lambda i: (i, 0))] * 3,
        out_specs=[VMEM] * 5,
        scratch_shapes=[pltpu.VMEM((PLANES, 16, SIDE), f32)],
        compiler_params=pltpu.CompilerParams(vmem_limit_bytes=60 << 20),
        name="pack",
    )(links, field, kx, ky, sea)


EVEN, ODD = slice(0, 128), slice(128, 256)
HALVES = (EVEN, ODD)


def sorter():
    col = lax.broadcasted_iota(jnp.int32, (SIDE, SIDE), 0)
    at = lax.broadcasted_iota(jnp.int32, (SIDE, SIDE), 1)
    want = jnp.where(at < 128, 2 * at, 2 * at - 255)
    return (col == want).astype(jnp.float32).astype(jnp.bfloat16)


def sort_columns(x, right):
    big = x.astype(jnp.bfloat16)
    small = (x - big.astype(jnp.float32)).astype(jnp.bfloat16)
    return jnp.dot(big, right, preferred_element_type=jnp.float32) + jnp.dot(
        small, right, preferred_element_type=jnp.float32
    )


def wide_weights(sea, kx, ky, rows, we, ww, wn):
    lane, sub = lanes(), sublanes()
    for t in range(rows):
        s = [sea(t, h) for h in range(2)]
        x = [kx(t, h) for h in range(2)]
        we[t, :, EVEN] = 0.5 * (x[0] + x[1]) * s[0] * s[1]
        w = 0.5 * (x[1] + roll(x[0], -1)) * s[1] * roll(s[0], -1)
        w = jnp.where(lane == 127, 0.0, w)
        we[t, :, ODD] = w
        ww[t] = roll(w, 1)
        for h in range(2):
            if t < rows - 1:
                sn, yn = sea(t + 1, h), ky(t + 1, h)
            else:
                sn, yn = up(sea(0, h)), up(ky(0, h))
            w = 0.5 * (ky(t, h) + yn) * s[h] * sn
            if t == rows - 1:
                w = jnp.where(sub == 7, 0.0, w)
            wn[t, :, HALVES[h]] = w


def wide_step(src, dst, we, ww, wn, rows, levels):
    below = []
    for l in levels:
        for h in HALVES:
            over = up(src[l, 0, :, h])
            src[l, rows, :, h] = over
            below.append(down(wn[rows - 1, :, h] * (over - src[l, rows - 1, :, h])))
    here = [src[l, 0, :, h] for l in levels for h in HALVES]
    for t in range(rows):
        e = [we[t, :, h] for h in HALVES]
        n = [wn[t, :, h] for h in HALVES]
        w = ww[t]
        nxt = [src[l, t + 1, :, h] for l in levels for h in HALVES]
        flux = [n[i % 2] * (nxt[i] - here[i]) for i in range(len(here))]
        for i, l in zip(range(0, len(here), 2), levels):
            a, b = here[i : i + 2]
            f = e[0] * (b - a)
            dst[l, t, :, EVEN] = (a + f) + w * (roll(b, 1) - a) + (flux[i] - below[i])
            dst[l, t, :, ODD] = (b - f) + e[1] * (roll(a, -1) - b) + (flux[i + 1] - below[i + 1])
        here, below = nxt, flux


def mixing(vertical):
    levels = vertical.shape[0]
    size = 16 * levels

    def at(shape, axis):
        return lax.broadcasted_iota(jnp.int32, shape, axis)


    def level(row):
        return LEV * (CHUNKS - 1 - row // (16 * LEV)) + row // 16 % LEV

    left = (level(at((size, levels), 0)) == at((size, levels), 1)).astype(jnp.float32).astype(jnp.bfloat16)
    right = (level(at((levels, size), 1)) == at((levels, size), 0)).astype(jnp.float32).astype(jnp.bfloat16)
    tall = jnp.dot(left, vertical, preferred_element_type=jnp.float32).astype(jnp.bfloat16)
    full = jnp.dot(tall, right, preferred_element_type=jnp.float32)
    same = at((size, size), 0) % 16 == at((size, size), 1) % 16
    return jnp.where(same, full, 0.0).astype(jnp.bfloat16)


def own_tile(low, high, i):
    group = lanes() // 32
    a, b = TILES[i]
    x = jnp.where(group == 0, roll(low[a], HALO), roll(high[a], 32 - 108))
    y = jnp.where(group == 2, roll(low[b], 64 + HALO), roll(high[b], 96 - 108))
    return jnp.where(group < 2, x, y)


def inner_kernel(*refs):
    field, kx, ky, sea = paired(refs[:8])
    vertical, cur, own, top, mixer, other, raw, st, we, ww, wn = refs[8:]
    for t in range(ROWS):
        low = planes_at(field, kx, ky, sea, t, 0)
        high = planes_at(field, kx, ky, sea, t, 1)
        for p in range(PLANES):
            raw[p, t, :, 0:128] = low[p]
            raw[p, t, :, 128:256] = high[p]
        for i in range(4):
            own[i, t] = own_tile(low, high, i)
    right = sorter()
    for p in range(PLANES):
        x = sort_columns(raw[p].reshape(SIDE, SIDE), right).reshape(ROWS, 8, SIDE)
        if p < LEV:
            cur[p, 0:ROWS] = x
        else:
            st[p - LEV] = x

    def plane(p):
        return lambda t, h: st[p, t, :, HALVES[h]]

    wide_weights(plane(0), plane(1), plane(2), ROWS, we, ww, wn)
    for h in range(2):
        cols = slice(128 * h, 128 * h + 128)
        land = sea[h][SIDE - TOP :, :].astype(jnp.float32)
        for l in range(LEV):
            top[l, :, cols] = field[h][l, SIDE - TOP :, :] * land
        top[LEV, :, cols] = land
        top[LEV + 1, :, cols] = kx[h][SIDE - TOP :, :]
        top[LEV + 2, :, cols] = ky[h][SIDE - TOP :, :]
    mixer[...] = mixing(vertical[...])

    def two_steps(_, none):
        wide_step(cur, other, we, ww, wn, ROWS, range(LEV))
        wide_step(other, cur, we, ww, wn, ROWS, range(LEV))
        return none

    lax.fori_loop(0, STEPS // 2, two_steps, 0)


def inner(field, kx, ky, sea, vertical):
    f32 = jnp.float32
    scratch = [
        (LEV, ROWS + 1, 8, SIDE),
        (PLANES, ROWS, 8, SIDE),
        (3, ROWS, 8, SIDE),
        (ROWS, 8, SIDE),
        (ROWS, 8, 128),
        (ROWS, 8, SIDE),
    ]
    shapes = [(LEV, ROWS + 1, 8, SIDE), (4, ROWS, 8, 128), (PLANES, TOP, SIDE)]
    return pl.pallas_call(
        inner_kernel,
        out_shape=[jax.ShapeDtypeStruct(s, f32) for s in shapes] + [jax.ShapeDtypeStruct((640, 640), jnp.bfloat16)],
        grid=(1,),
        in_specs=half_specs((LEV,), (), (), ()) + [VMEM],
        out_specs=[VMEM] * 4,
        scratch_shapes=[pltpu.VMEM(s, f32) for s in scratch],
        compiler_params=pltpu.CompilerParams(vmem_limit_bytes=24 << 20),
        cost_estimate=pl.CostEstimate(flops=40_000_000, bytes_accessed=40_000_000, transcendentals=0),
        name="inner",
    )(*doubled(field, kx, ky, sea), vertical)


def strip_step(src, dst, we, ww, wn, tiles):
    sub = sublanes()
    below = []
    for k in tiles:
        over = jnp.where(sub == 7, src[k, ROWS], up(src[k, 0]))
        src[k, ROWS] = over
        below.append(jnp.where(sub == 0, 0.0, down(wn[ROWS - 1] * (over - src[k, ROWS - 1]))))
    here = [src[k, 0] for k in tiles]
    for t in range(STRIP):
        e, w, n = we[t], ww[t], wn[t]
        nxt = [src[k, t + 1] for k in tiles]
        flux = [n * (x - c) for x, c in zip(nxt, here)]
        for k, c, f, g in zip(tiles, here, flux, below):
            dst[k, t] = c + e * (roll(c, -1) - c) + w * (roll(c, 1) - c) + (f - g)
        here, below = nxt, flux


def rim_kernel(links, inside, own, top, west, east, north, nw, ne, out, cur, other, we, ww, wn, kap, sea, ext, nbr, nb_even, nb_odd, nc, n_other, nwe, nww, nwn):
    lane, sub = lanes(), sublanes()
    group, part = lane // 32, lane % 32
    w_halo = (part < HALO) & (group % 2 == 0)
    e_halo = (part >= 20) & (group % 2 == 1)
    ones = jnp.ones((8, 128), jnp.float32)

    def with_halo(i, mine, w, e):
        x = jnp.where(w_halo, roll(w, W_SHIFT[i]), mine)
        return jnp.where(e_halo, roll(e, E_SHIFT[i]), x)

    strips = (cur.at[0], cur.at[1], cur.at[2], kap)
    def fill(b, none):
        for j in range(8):
            t = 8 * b + j
            at = pl.ds(t, 8, stride=ROWS)
            w, e = west[at, :], east[at, :]
            for i in range(4):
                strips[i][t] = with_halo(i, own[i, t], w, e)
        return none

    lax.fori_loop(0, ROWS // 8, fill, 0)
    for o in range(2):
        rows = slice(8 * o, 8 * o + 8)
        low = [north[p, rows, 0:128] for p in range(PLANES)]
        high = [north[p, rows, 128:256] for p in range(PLANES)]
        for i in range(4):
            ext[i, rows, :] = with_halo(i, own_tile(low, high, i), nw[rows, :], ne[rows, :])
    for k in range(DEPTH):
        for i in range(4):
            strips[i][ROWS + k] = jnp.broadcast_to(ext[i, k : k + 1, :], (8, 128))

    def flag(x):
        return jnp.where(x >= 0, 1.0, 0.0).astype(jnp.float32)

    w_open = ones * flag(links[0, 0])
    e_open = ones * flag(links[0, 1])
    w_over = jnp.broadcast_to(north[LEV, 15:16, 0:128], (8, 128))
    e_over = jnp.broadcast_to(north[LEV, 14:15, 0:128], (8, 128))
    seams = []
    for a, b in ((w_open, e_open), (w_over, e_over)):
        m = jnp.where(lane == HALO - 1, a, jnp.where(lane == 32 + 19, b, 1.0))
        seams.append(0.5 * jnp.where(part == 31, 0.0, m))
    first = group < 2
    def spread_sea(b, none):
        for j in range(14):
            c = cur[2, 14 * b + j]
            sea[14 * b + j] = jnp.where(first, roll(c, 64), c)
        return none

    lax.fori_loop(0, STRIP // 14, spread_sea, 0)

    def weights(t, seam, s, x, sn, yn):
        w = seam * (x + roll(x, -1)) * s * roll(s, -1)
        w = jnp.where(first, w, roll(w, 64))
        we[t] = w
        ww[t] = roll(w, 1)
        w = 0.5 * (x + yn) * s * sn
        wn[t] = jnp.where(first, roll(w, 64), w)

    def most_weights(b, none):
        for j in range(14):
            t = 14 * b + j
            weights(t, seams[0], sea[t], kap[t], sea[t + 1], kap[t + 1])
        return none

    lax.fori_loop(0, 2, most_weights, 0)
    for t in range(28, STRIP):
        s, x = sea[t], kap[t]
        sn, yn = (sea[t + 1], kap[t + 1]) if t < STRIP - 1 else (s, x)
        if t == ROWS - 1:
            sn = jnp.where(sub == 7, sn, up(sea[0]))
            yn = jnp.where(sub == 7, yn, up(kap[0]))
        weights(t, seams[t >= ROWS], s, x, sn, yn)
    zeros = jnp.zeros((8, 128), jnp.float32)
    wn[STRIP - 1] = zeros
    for i in range(3):
        cur[i, STRIP] = zeros
        other[i, STRIP] = zeros

    nbr[:, 0:TOP, :] = top[...]
    nbr[:, TOP : TOP + 16, :] = north[...]
    x = sort_columns(nbr[...].reshape(PLANES * (TOP + 16), SIDE), sorter()).reshape(PLANES, TOP + 16, SIDE)
    nb = (nb_even, nb_odd)
    for h in range(2):
        nb[h][...] = x[:, :, HALVES[h]]
    for l in range(LEV):
        for t in range(NORTH):
            for h in range(2):
                nc[l, t, :, HALVES[h]] = strided(nb, (l,), t, h, NORTH)

    def plane(p):
        return lambda t, h: strided(nb, (p,), t, h, NORTH)

    wide_weights(plane(LEV), plane(LEV + 1), plane(LEV + 2), NORTH, nwe, nww, nwn)

    def two_steps(_, none):
        strip_step(cur, other, we, ww, wn, range(3))
        wide_step(nc, n_other, nwe, nww, nwn, NORTH, range(LEV))
        strip_step(other, cur, we, ww, wn, range(3))
        wide_step(n_other, nc, nwe, nww, nwn, NORTH, range(LEV))
        return none

    lax.fori_loop(0, STEPS // 2, two_steps, 0)

    for l in range(LEV):
        for t in range(NORTH):
            for h in range(2):
                nb[h][l, pl.ds(t, 8, stride=NORTH), :] = nc[l, t, :, HALVES[h]]

    on_rim = (lane < 5) | (lane >= 123)
    top_row = sub == 7
    for l in range(LEV):
        i, base = l // 2, 64 * (l % 2)
        pick = [
            jnp.where(lane < 5, base + HALO + 2 * lane + h, jnp.where(lane >= 123, base + 42 + 2 * (lane - 123) + h, 0))
            for h in range(2)
        ]
        for t in range(0, ROWS, 2):
            pair = []
            for u in (t, t + 1):
                for h in range(2):
                    x = inside[l, u, :, HALVES[h]]
                    if u >= ROWS - DEPTH:
                        r = TOP - ROWS + u
                        x = jnp.where(top_row, jnp.broadcast_to(nb[h][l, r : r + 1, :], (8, 128)), x)
                    pair.append(jnp.where(on_rim, jnp.take_along_axis(cur[i, u], pick[h], axis=1), x))
            q, r = t // 4, 8 * (t % 4)
            for h in range(2):
                x = jnp.concatenate([pair[h], pair[2 + h]], axis=0)
                out[q, l, r : r + 16, HALVES[h]] = x.astype(jnp.bfloat16)


def rim(links, inside, own, top, west, east, north, nw, ne):
    f32 = jnp.float32
    scratch = [
        (3, STRIP + 1, 8, 128),
        (3, STRIP + 1, 8, 128),
        (STRIP, 8, 128),
        (STRIP, 8, 128),
        (STRIP, 8, 128),
        (STRIP, 8, 128),
        (STRIP, 8, 128),
        (4, 16, 128),
        (PLANES, TOP + 16, SIDE),
        (PLANES, TOP + 16, 128),
        (PLANES, TOP + 16, 128),
        (LEV, NORTH + 1, 8, SIDE),
        (LEV, NORTH + 1, 8, SIDE),
        (NORTH, 8, SIDE),
        (NORTH, 8, 128),
        (NORTH, 8, SIDE),
    ]
    return pl.pallas_call(
        rim_kernel,
        out_shape=jax.ShapeDtypeStruct((CHUNKS, LEV, SIDE // CHUNKS, SIDE), jnp.bfloat16),
        in_specs=[SMEM] + [VMEM] * 8,
        out_specs=VMEM,
        scratch_shapes=[pltpu.VMEM(s, f32) for s in scratch],
        compiler_params=pltpu.CompilerParams(vmem_limit_bytes=24 << 20),
        name="rim",
    )(links, inside, own, top, west, east, north, nw, ne)


def mix_kernel(x, k, y):
    for h in range(2):
        rows = x[:, :, 16 * h : 16 * h + 16, :].reshape(CHUNKS * LEV * 16, SIDE)
        mixed = jnp.dot(k[...], rows, preferred_element_type=jnp.float32).astype(jnp.bfloat16)
        y[:, :, 16 * h : 16 * h + 16, :] = mixed.reshape(CHUNKS, LEV, 16, SIDE)


def mix(x, k):
    return pl.pallas_call(
        mix_kernel,
        out_shape=jax.ShapeDtypeStruct(x.shape, jnp.bfloat16),
        in_specs=[VMEM] * 2,
        out_specs=VMEM,
        compiler_params=pltpu.CompilerParams(vmem_limit_bytes=24 << 20),
        name="mix",
    )(x, k)


def unpack_kernel(z, out):
    at = lax.broadcasted_iota(jnp.int32, (SIDE, 128), 0)
    col = lax.broadcasted_iota(jnp.int32, (SIDE, 128), 1) + 128 * pl.program_id(0)
    back = (jnp.where(at < 128, 2 * at, 2 * at - 255) == col).astype(jnp.float32).astype(jnp.bfloat16)
    for q in range(CHUNKS):
        x = jnp.dot(z[q].reshape(LEV * 32, SIDE), back, preferred_element_type=jnp.float32)
        for l in range(LEV):
            for u in range(4):
                r = 32 * l + 8 * u
                out[l, pl.ds(4 * q + u, 8, stride=ROWS), :] = x[r : r + 8]


def unpack(z):
    return pl.pallas_call(
        unpack_kernel,
        out_shape=jax.ShapeDtypeStruct((LEV, SIDE, SIDE), jnp.float32),
        grid=(2,),
        in_specs=[VMEM],
        out_specs=pl.BlockSpec((LEV, SIDE, 128), lambda h: (0, 0, h)),
        compiler_params=pltpu.CompilerParams(vmem_limit_bytes=24 << 20),
        name="unpack",
    )(z)


def shards(field, kappa_x, kappa_y, sea_mask, tile_links, vertical):
    tiles = lax.axis_size("tile")

    def send(x, target):
        return lax.ppermute(x, "tile", [(i, target(i) % tiles) for i in range(tiles)])

    cells, kx, ky, sea = field[0], kappa_x[0], kappa_y[0], sea_mask[0]
    west, east, north, nw, ne = pack(tile_links, cells, kx, ky, sea)
    from_east = send(west, lambda i: i - 1)
    from_west = send(east, lambda i: i + 1)
    from_north = send(north, lambda i: -i)
    from_nw = send(nw, lambda i: 1 - i)
    from_ne = send(ne, lambda i: -1 - i)
    inside, own, top, mixer = inner(cells, kx, ky, sea, vertical)
    smooth = rim(tile_links, inside, own, top, from_west, from_east, from_north, from_nw, from_ne)

    def turn(x):
        return lax.all_to_all(x, "lev", 0, 0, axis_index_groups=[list(range(CHUNKS))[::-1]], tiled=True)

    return unpack(turn(mix(turn(smooth), mixer)))[None]


def solution(mesh):
    placed = (
        P("tile", "lev", None, None),
        P("tile", None, None),
        P("tile", None, None),
        P("tile", None, None),
        P("tile", None),
        P(),
    )
    return jax.shard_map(
        shards, mesh=mesh, in_specs=placed, out_specs=P("tile", "lev", None, None), check_vma=False
    )
```
